32 devices in a mesh: grp: 2 (over y), sp: 4 (over z), sec: 2 (over x), mb: 2 (over core).
Axes of the slice: x: 2, y: 2, z: 4, core: 2. Of those that a mesh axis runs over, the one named last changes fastest.
Arguments:
- atmosphere: bfloat16 [8, 24, 32, 256], P(('grp', 'mb'), None, 'sp', 'sec'), parts along dimension 0, may hold values from -6 to 6
- ocean_state: bfloat16 [8, 8, 32, 128], P(('grp', 'mb'), None, 'sp'), parts along dimension 0, may hold values from -6 to 6
- fluxes: bfloat16 [8, 8, 32, 128], P(('grp', 'mb'), None, 'sp'), parts along dimension 0, may hold values from -6 to 6
- sea_mask: int32 [32, 128], P('sp'), may hold values 0 or 1
- air_entry: bfloat16 [3, 3, 32, 136], replicated, may hold values from -0.375 to 0.375
- air_middle: bfloat16 [3, 3, 136, 136], replicated, may hold values from -0.15625 to 0.15625
- air_exit: bfloat16 [3, 3, 136, 32], replicated, may hold values from -0.15625 to 0.15625
- sea_entry: bfloat16 [3, 3, 16, 136], replicated, may hold values from -0.5 to 0.5
- sea_exit: bfloat16 [3, 3, 136, 8], replicated, may hold values from -0.15625 to 0.15625
Outputs:
- air_final: bfloat16 [8, 24, 32, 256], P(('grp', 'mb'), None, 'sp', 'sec'), parts along dimension 0
- sea_final: bfloat16 [8, 8, 32, 128], P(('grp', 'mb'), None, 'sp'), parts along dimension 0
The draws below stay inside these ranges and needn't reach their ends.
There are 2 independent parts, one for each index of `grp`. The reference program is written for one: setup_inputs(seed, part) draws one part's arguments, and reference() takes and returns one part's arrays. A program takes and returns all parts, laid end to end along the dimension named above; an argument that names none is the same for every part. Nothing has to cross between parts.
All inputs are finite; a program needn't handle non-finite values. No bound on the sum of `sea_mask` on one device may be relied on, other than what follows from the above.
Results may differ from the reference program's by a relative error of at most 0.0055.
Values may be sent and summed in bfloat16 or wider, within the bound.
A program may use at most 64 MiB of HBM per device.

```python
import jax
import jax.numpy as jnp
from jax import lax

FIELDS = 24
SURFACE = 8
FLUX = 8
HIDDEN_SIZE = 136
STEPS = 2
MEMBERS = 4
ROWS = 32
OCEAN_COLS = 128
AIR_COLS = 256


def touch_ends(values, own_key, least, largest):
    extent = values.shape
    index_at = [jax.random.randint(jax.random.fold_in(own_key, axis), (), 0, extent[axis]) for axis in range(len(extent))]
    values = values.at[tuple(index_at)].set(least)
    longest = extent.index(max(extent))
    index_at[longest] = (index_at[longest] + 1) % extent[longest]
    return values.at[tuple(index_at)].set(largest)


def block_scale(stream_key, shape, shards, low, top_value):
    loudness = 1.0
    for dim, shards_of in shards:
        steps = jax.random.uniform(jax.random.fold_in(jax.random.fold_in(stream_key, 6), dim), (shards_of,), jnp.float32, low / len(shards), top_value / len(shards))
        loudness = loudness * jnp.repeat(jnp.exp(steps), shape[dim] // shards_of).reshape((-1,) + (1,) * (len(shape) - 1 - dim))
    return loudness


def gaussian(rng, dims, scale, limit, cuts=(), held_as=jnp.bfloat16):
    level = block_scale(rng, dims, cuts, -0.22, 0.18) if cuts else 1.0
    drawn = jax.random.normal(rng, dims, jnp.float32) * scale * level
    return jnp.minimum(jnp.maximum(drawn, -limit), limit).astype(held_as)


def setup_inputs(seed: int = 0, part: int = 0) -> dict:
    keys = jax.random.split(jax.random.key(seed), 10)
    part_splits = jax.random.split(jax.random.fold_in(keys[9], part), 10)
    return {
        "atmosphere": gaussian(part_splits[0], (MEMBERS, FIELDS, ROWS, AIR_COLS), 1.0, 6.0, ((0, 2), (2, 4), (3, 2))),
        "ocean_state": gaussian(part_splits[1], (MEMBERS, SURFACE, ROWS, OCEAN_COLS), 1.0, 6.0, ((0, 2), (2, 4))),
        "fluxes": gaussian(part_splits[2], (MEMBERS, FLUX, ROWS, OCEAN_COLS), 1.0, 6.0, ((0, 2), (2, 4))),
        "sea_mask": touch_ends((jax.random.randint(keys[3], (ROWS, OCEAN_COLS), 0, 3) < 2).astype(jnp.int32), jax.random.fold_in(keys[3], 1), 0, 1),
        "air_entry": gaussian(keys[4], (3, 3, FIELDS + SURFACE, HIDDEN_SIZE), (9 * (FIELDS + SURFACE)) ** -0.5, 0.375),
        "air_middle": gaussian(keys[5], (3, 3, HIDDEN_SIZE, HIDDEN_SIZE), (9 * HIDDEN_SIZE) ** -0.5, 0.15625),
        "air_exit": gaussian(keys[6], (3, 3, HIDDEN_SIZE, FIELDS + FLUX), (9 * HIDDEN_SIZE) ** -0.5, 0.15625),
        "sea_entry": gaussian(keys[7], (3, 3, SURFACE + FLUX, HIDDEN_SIZE), (9 * (SURFACE + FLUX)) ** -0.5, 0.5),
        "sea_exit": gaussian(keys[8], (3, 3, HIDDEN_SIZE, SURFACE), (9 * HIDDEN_SIZE) ** -0.5, 0.15625),
    }


def wrap_rows(field, spread):
    return jnp.concatenate([field[:, -spread:], field, field[:, :spread]], axis=1)


def pad_columns(field, spread):
    return jnp.pad(field, ((0, 0), (0, 0), (spread, spread)))


def convolve(field, weight, dilation):
    wrapped = wrap_rows(field, dilation)
    produced = lax.conv_general_dilated(wrapped[None], weight.astype(jnp.float32), (1, 1), "VALID", rhs_dilation=(dilation, dilation), dimension_numbers=("NCHW", "HWIO", "NCHW"), precision=lax.Precision.HIGHEST)
    return produced[0]


def sea_member(state, flux_now, sea_weight, sea_entry, sea_exit):
    entry = jnp.concatenate([state, flux_now], axis=0).astype(jnp.float32)
    hidden = jax.nn.gelu(convolve(pad_columns(entry, 1), sea_entry, 1), approximate=True).astype(jnp.bfloat16)
    hidden = lax.optimization_barrier(hidden)
    produced = convolve(pad_columns(hidden.astype(jnp.float32), 1), sea_exit, 1)
    return (state.astype(jnp.float32) + sea_weight * produced).astype(jnp.bfloat16)


def air_member(state, surface_now, air_entry, air_middle, air_exit):
    extra_cols = AIR_COLS - OCEAN_COLS
    surface_wide = jnp.concatenate([surface_now, jnp.zeros((SURFACE, ROWS, extra_cols), surface_now.dtype)], axis=2)
    entry = jnp.concatenate([state, surface_wide], axis=0).astype(jnp.float32)
    hidden = convolve(pad_columns(entry, 1), air_entry, 1)[:, :, :OCEAN_COLS]
    hidden = jax.nn.gelu(hidden, approximate=True).astype(jnp.bfloat16)
    hidden = lax.optimization_barrier(hidden)
    hidden = jax.nn.gelu(convolve(pad_columns(hidden.astype(jnp.float32), 2), air_middle, 2), approximate=True).astype(jnp.bfloat16)
    hidden = lax.optimization_barrier(hidden)
    produced = convolve(pad_columns(hidden.astype(jnp.float32), 4), air_exit, 4)
    renewed = (state[:, :, :OCEAN_COLS].astype(jnp.float32) + produced[:FIELDS]).astype(jnp.bfloat16)
    new_state = jnp.concatenate([renewed, state[:, :, OCEAN_COLS:]], axis=2)
    return new_state, produced[FIELDS:].astype(jnp.bfloat16)


def reference(atmosphere, ocean_state, fluxes, sea_mask, air_entry, air_middle, air_exit, sea_entry, sea_exit):
    sea_weight = sea_mask.astype(jnp.float32)

    def one_member(members):
        state, sea_now, flux_now = members
        for step_index in range(STEPS):
            sea_now = sea_member(sea_now, flux_now, sea_weight, sea_entry, sea_exit)
            state, flux_now = air_member(state, sea_now, air_entry, air_middle, air_exit)
        return state, sea_now

    air_final, sea_final = lax.map(one_member, (atmosphere, ocean_state, fluxes))
    return air_final, sea_final
```

```python
import functools

import jax
import jax.numpy as jnp
from jax import lax
from jax.experimental import pallas as pl
from jax.experimental.pallas import tpu as pltpu
from jax.sharding import PartitionSpec as P

STEPS = 2
SEA_DILATIONS = (1, 1)
AIR_DILATIONS = (1, 2, 4)
LANES = 128
MESH = pl.DeviceIdType.MESH
F32 = jnp.float32
BF16 = jnp.bfloat16


def round_up(value, unit):
    return -(-value // unit) * unit


def rounded(value):
    return value.astype(BF16).astype(F32)


def gelu(v):
    return 0.5 * v * (1.0 + jnp.tanh(0.7978845608028654 * (v + 0.044715 * (v * v * v))))


def kernel(
    dims,
    atm_ref, sea_ref, flux_ref, mask_ref, w_air1, w_air2, w_air3, w_sea1, w_sea2,
    air_out, sea_out,
    got_atm, got_sea, got_flux, got_mask, got_edge, edge_src,
    atm_f, sea_f, flux_f, mask_f, edge_p, hidden_a, hidden_b,
    stage, stage_sea, fin_air_src, fin_air, fin_sea_src, fin_sea,
    atm_send, atm_recv, near_send, near_recv, edge_send, edge_recv,
    fin_air_send, fin_air_recv, fin_sea_send, fin_sea_recv,
):
    sp, sections, members, rows, fields, surface, cols, window, home, hidden = dims
    bands = sections - 1
    total = window * rows
    own = home * rows
    me = lax.axis_index("sp")
    sec = lax.axis_index("sec")
    member = lax.rem(sec, members)
    base = sec - member
    in_band = sec < bands

    def target_row(slot):
        return lax.rem(me - slot + home + 2 * sp, sp)

    lane = lax.broadcasted_iota(jnp.int32, (fields, LANES), 1)

    @pl.when(sec == bands)
    def _():
        for m in range(members):
            stage[0] = atm_ref[m].astype(F32)
            tile = jnp.zeros((fields, LANES), F32)
            for r in range(rows):
                line = stage[0, pl.ds(r, fields, stride=rows), :]
                line = line if r == 0 else pltpu.roll(line, r, 1)
                tile = jnp.where(lane == r, line, tile)
            edge_src[m] = jnp.concatenate(
                [tile, jnp.zeros((surface, LANES), F32)], axis=0
            ).astype(BF16)
        got_edge[home] = edge_src[member]

    @pl.when(in_band)
    def _():
        got_atm[home, jnp.minimum(sec, bands - 1)] = atm_ref[member]

    got_sea[home] = sea_ref[member]
    got_flux[home] = flux_ref[member]
    got_mask[home] = mask_ref[...]

    barrier = pltpu.get_barrier_semaphore()
    for slot in range(window):
        for to in range(sections):
            far = slot != home

            def greet(slot=slot, to=to):
                pl.semaphore_signal(
                    barrier, inc=1, device_id={"sp": target_row(slot), "sec": to},
                    device_id_type=MESH,
                )

            if far:
                greet()
            else:
                pl.when(sec != to)(greet)
    pl.semaphore_wait(barrier, window * sections - 1)

    def near_copies(slot):
        place = {"sp": target_row(slot), "sec": sec}
        pairs = (
            (sea_ref.at[member], got_sea.at[slot]),
            (flux_ref.at[member], got_flux.at[slot]),
            (mask_ref, got_mask.at[slot]),
        )
        return [
            pltpu.make_async_remote_copy(
                src_ref=src, dst_ref=dst,
                send_sem=near_send.at[slot, k], recv_sem=near_recv.at[slot, k],
                device_id=place, device_id_type=MESH,
            )
            for k, (src, dst) in enumerate(pairs)
        ]

    def atm_copy(slot, to, band):
        return pltpu.make_async_remote_copy(
            src_ref=atm_ref.at[to % members], dst_ref=got_atm.at[slot, band],
            send_sem=atm_send.at[slot, to], recv_sem=atm_recv.at[slot, band],
            device_id={"sp": target_row(slot), "sec": to}, device_id_type=MESH,
        )

    def edge_copy(slot, to):
        return pltpu.make_async_remote_copy(
            src_ref=edge_src.at[to % members], dst_ref=got_edge.at[slot],
            send_sem=edge_send.at[slot, to], recv_sem=edge_recv.at[slot],
            device_id={"sp": target_row(slot), "sec": to}, device_id_type=MESH,
        )

    slots = sorted(range(window), key=lambda slot: -abs(slot - home))
    for slot in slots:
        if slot != home:
            for copy in near_copies(slot):
                copy.start()

    def each_target(act):
        for slot in slots:
            for to in range(sections):
                if slot == home:
                    pl.when(sec != to)(functools.partial(act, slot, to))
                else:
                    act(slot, to)

    @pl.when(in_band)
    def _():
        band = jnp.minimum(sec, bands - 1)
        each_target(lambda slot, to: atm_copy(slot, to, band).start())

    @pl.when(sec == bands)
    def _():
        each_target(lambda slot, to: edge_copy(slot, to).start())

    column = lax.broadcasted_iota(jnp.int32, (1, cols), 1)
    tile_rows = max(1, 512 // cols)

    def span(margin):
        count = round_up(rows + 2 * margin, tile_rows)
        if count >= total:
            return 0, total
        return own - margin, count

    def conv(load, weight_ref, outs, dilation, margin, emit):
        start, count = span(margin)

        def step(i, carry):
            first = start + i * tile_rows + 2 * total
            pieces = []
            lines = []
            for t in range(tile_rows):
                lines.append(lax.rem(first + t, total))
                taps = [load(lax.rem(first + t + (a - 1) * dilation, total)) for a in range(3)]
                pieces.append(jnp.concatenate(taps, axis=0))
            block = pieces[0] if tile_rows == 1 else jnp.concatenate(pieces, axis=1)
            made = jnp.dot(weight_ref[...], block, preferred_element_type=F32)
            for t in range(tile_rows):
                part = made[:, t * cols:(t + 1) * cols]
                left = pltpu.roll(part[:outs], dilation, 1)
                right = pltpu.roll(part[2 * outs:3 * outs], cols - dilation, 1)
                value = part[outs:2 * outs]
                value = value + jnp.where(column >= dilation, left, 0.0)
                value = value + jnp.where(column < cols - dilation, right, 0.0)
                emit(lines[t], value)
            return carry

        lax.fori_loop(0, count // tile_rows, step, 0)

    def load_sea(r):
        return jnp.concatenate([sea_f[r], flux_f[r]], axis=0).astype(BF16)

    def load_air(r):
        return jnp.concatenate([atm_f[r], sea_f[r]], axis=0).astype(BF16)

    def keep(ref):
        def emit(r, value):
            made = gelu(value)
            spare = jnp.zeros((ref.shape[1] - hidden, cols), F32)
            ref[r] = jnp.concatenate([made, spare], axis=0).astype(BF16)
        return emit

    def emit_sea(r, value):
        sea_f[r] = rounded(sea_f[r] + mask_f[r] * value)

    last_lane = lax.broadcasted_iota(jnp.int32, (hidden, LANES), 1) == LANES - 1

    def emit_air1(r, value):
        rim = jnp.where(last_lane, pltpu.roll(edge_p[...], LANES - 1 - r, 1), 0.0)
        if cols > LANES:
            rim = jnp.concatenate([jnp.zeros((hidden, cols - LANES), F32), rim], axis=1)
        keep(hidden_a)(r, value + rim)

    def emit_air3(r, value):
        atm_f[r] = rounded(atm_f[r] + value[:fields])
        flux_f[r] = rounded(value[fields:])

    for slot in range(window):
        if slot != home:
            for copy in near_copies(slot):
                copy.wait_recv()
        for k, (got, state) in enumerate(((got_sea, sea_f), (got_flux, flux_f))):
            for band in range(bands):
                part = slice(band * LANES, (band + 1) * LANES)
                stage_sea[band] = got[slot, :, part].astype(F32)
                for r in range(rows):
                    state[slot * rows + r, :, part] = stage_sea[
                        band, pl.ds(r, surface, stride=rows), :
                    ]
        weight = got_mask[slot].astype(F32)
        for r in range(rows):
            mask_f[slot * rows + r] = jnp.broadcast_to(weight[r:r + 1], (surface, cols))

    def take_atmosphere():
        for slot in range(window):
            for band in range(bands):
                if slot == home:
                    pl.when(sec != band)(lambda: atm_copy(slot, 0, band).wait_recv())
                else:
                    atm_copy(slot, 0, band).wait_recv()
                stage[band] = got_atm[slot, band].astype(F32)
                for r in range(rows):
                    atm_f[slot * rows + r, :, band * LANES:(band + 1) * LANES] = stage[
                        band, pl.ds(r, fields, stride=rows), :
                    ]
            if slot == home:
                pl.when(sec != bands)(lambda: edge_copy(slot, 0).wait_recv())
            else:
                edge_copy(slot, 0).wait_recv()
        place = lax.broadcasted_iota(jnp.int32, (fields + surface, LANES), 1)
        edge = jnp.zeros((fields + surface, LANES), F32)
        for slot in range(window):
            part = got_edge[slot].astype(F32)
            edge = edge + (part if slot == 0 else pltpu.roll(part, slot * rows, 1))
        above = jnp.where(
            place == 0, pltpu.roll(edge, LANES - (total - 1), 1), pltpu.roll(edge, 1, 1)
        )
        below = jnp.where(
            place == total - 1, pltpu.roll(edge, total - 1, 1), pltpu.roll(edge, LANES - 1, 1)
        )
        three = jnp.concatenate([above, edge, below], axis=0).astype(BF16)
        edge_p[...] = jnp.dot(
            w_air1[2 * hidden:3 * hidden, :], three, preferred_element_type=F32
        )

    halo = sum(SEA_DILATIONS) + sum(AIR_DILATIONS)
    for step in range(STEPS):
        after = (STEPS - 1 - step) * halo
        air = sum(AIR_DILATIONS)
        conv(load_sea, w_sea1, hidden, 1, after + air + 1, keep(hidden_a))
        conv(lambda r: hidden_a[r], w_sea2, surface, 1, after + air, emit_sea)
        if step == STEPS - 1:
            for band in range(bands):
                part = slice(band * LANES, (band + 1) * LANES)
                for r in range(rows):
                    stage_sea[band, pl.ds(r, surface, stride=rows), :] = sea_f[own + r, :, part]
                fin_sea_src[:, part] = stage_sea[band].astype(BF16)
            sea_copies = []
            for k in range(1, members):
                to = lax.rem(member + k, members)
                sea_copies.append(pltpu.make_async_remote_copy(
                    src_ref=fin_sea_src, dst_ref=fin_sea.at[member],
                    send_sem=fin_sea_send.at[k], recv_sem=fin_sea_recv.at[member],
                    device_id={"sec": base + to}, device_id_type=MESH,
                ))
                sea_copies[-1].start()
        if step == 0:
            take_atmosphere()
        conv(load_air, w_air1, hidden, 1, after + 6, emit_air1)
        conv(lambda r: hidden_a[r], w_air2, hidden, 2, after + 4, keep(hidden_b))
        conv(lambda r: hidden_b[r], w_air3, fields + surface, 4, after, emit_air3)

    for band in range(bands):
        for r in range(rows):
            stage[band, pl.ds(r, fields, stride=rows), :] = atm_f[
                own + r, :, band * LANES:(band + 1) * LANES
            ]
        fin_air_src[band] = stage[band].astype(BF16)

    def air_copy(k, landing):
        to = base + lax.rem(member + k, members)
        return to, pltpu.make_async_remote_copy(
            src_ref=fin_air_src.at[jnp.minimum(to, bands - 1)], dst_ref=fin_air.at[landing],
            send_sem=fin_air_send.at[k], recv_sem=fin_air_recv.at[landing],
            device_id={"sec": to}, device_id_type=MESH,
        )

    for k in range(1, members):
        to, copy = air_copy(k, member)
        pl.when(to < bands)(copy.start)

    sea_out[member] = fin_sea_src[...]
    for k in range(1, members):
        origin = lax.rem(member + k, members)
        pltpu.make_async_remote_copy(
            src_ref=fin_sea_src, dst_ref=fin_sea.at[origin],
            send_sem=fin_sea_send.at[k], recv_sem=fin_sea_recv.at[origin],
            device_id={"sec": base + origin}, device_id_type=MESH,
        ).wait_recv()
        sea_out[origin] = fin_sea[origin]

    @pl.when(sec == bands)
    def _():
        air_out[...] = atm_ref[...]

    @pl.when(in_band)
    def _():
        air_out[member] = fin_air_src[jnp.minimum(sec, bands - 1)]
        for k in range(1, members):
            origin = lax.rem(member + k, members)
            air_copy(k, origin)[1].wait_recv()
            air_out[origin] = fin_air[origin]

    for copy in sea_copies:
        copy.wait_send()
    for k in range(1, members):
        to, copy = air_copy(k, member)
        pl.when(to < bands)(copy.wait_send)
    for slot in slots:
        if slot != home:
            for copy in near_copies(slot):
                copy.wait_send()

    @pl.when(in_band)
    def _():
        band = jnp.minimum(sec, bands - 1)
        each_target(lambda slot, to: atm_copy(slot, to, band).wait_send())

    @pl.when(sec == bands)
    def _():
        each_target(lambda slot, to: edge_copy(slot, to).wait_send())


def flat_weight(weight):
    depth, outs = weight.shape[2:]
    padded = jnp.pad(weight, ((0, 0), (0, 0), (0, round_up(depth, 16) - depth), (0, 0)))
    return padded.transpose(1, 3, 0, 2).reshape(3 * outs, -1)


def shards(
    atmosphere, ocean_state, fluxes, sea_mask, air_entry, air_middle, air_exit, sea_entry, sea_exit
):
    sp = lax.axis_size("sp")
    sections = lax.axis_size("sec")
    bands = sections - 1
    members, fields, rows, band_cols = atmosphere.shape
    surface, cols = ocean_state.shape[1], ocean_state.shape[3]
    hidden = air_entry.shape[3]
    reach = STEPS * (sum(SEA_DILATIONS) + sum(AIR_DILATIONS))
    window = min(sp, 2 * (-(-reach // rows)) + 1)
    home = (window - 1) // 2
    total = window * rows
    depth = round_up(hidden, 16)
    assert band_cols == LANES and cols == bands * band_cols
    assert sections % members == 0 and total <= LANES and surface == fluxes.shape[1]
    dims = (sp, sections, members, rows, fields, surface, cols, window, home, hidden)
    dma = pltpu.SemaphoreType.DMA
    flat = fields * rows
    flat_sea = surface * rows
    air, sea = pl.pallas_call(
        functools.partial(kernel, dims),
        out_shape=(
            jax.ShapeDtypeStruct((members, flat, band_cols), BF16),
            jax.ShapeDtypeStruct((members, flat_sea, cols), BF16),
        ),
        in_specs=[pl.BlockSpec(memory_space=pltpu.VMEM)] * 9,
        out_specs=(pl.BlockSpec(memory_space=pltpu.VMEM),) * 2,
        scratch_shapes=[
            pltpu.VMEM((window, bands, flat, LANES), BF16),
            pltpu.VMEM((window, flat_sea, cols), BF16),
            pltpu.VMEM((window, flat_sea, cols), BF16),
            pltpu.VMEM((window, rows, cols), jnp.int32),
            pltpu.VMEM((window, fields + surface, LANES), BF16),
            pltpu.VMEM((members, fields + surface, LANES), BF16),
            pltpu.VMEM((total, fields, cols), F32),
            pltpu.VMEM((total, surface, cols), F32),
            pltpu.VMEM((total, surface, cols), F32),
            pltpu.VMEM((total, surface, cols), F32),
            pltpu.VMEM((hidden, LANES), F32),
            pltpu.VMEM((total, depth, cols), BF16),
            pltpu.VMEM((total, depth, cols), BF16),
            pltpu.VMEM((bands, flat, LANES), F32),
            pltpu.VMEM((bands, flat_sea, LANES), F32),
            pltpu.VMEM((bands, flat, LANES), BF16),
            pltpu.VMEM((members, flat, LANES), BF16),
            pltpu.VMEM((flat_sea, cols), BF16),
            pltpu.VMEM((members, flat_sea, cols), BF16),
            dma((window, sections)),
            dma((window, bands)),
            dma((window, 3)),
            dma((window, 3)),
            dma((window, sections)),
            dma((window,)),
            dma((members,)),
            dma((members,)),
            dma((members,)),
            dma((members,)),
        ],
        compiler_params=pltpu.CompilerParams(
            collective_id=0, has_side_effects=True, vmem_limit_bytes=48 * 1024 * 1024
        ),
    )(
        atmosphere.reshape(members, flat, band_cols),
        ocean_state.reshape(members, flat_sea, cols),
        fluxes.reshape(members, flat_sea, cols),
        sea_mask,
        flat_weight(air_entry),
        flat_weight(air_middle),
        flat_weight(air_exit),
        flat_weight(sea_entry),
        flat_weight(sea_exit),
    )
    return air.reshape(atmosphere.shape), sea.reshape(ocean_state.shape)


def solution(mesh):
    placed = (
        P(("grp", "mb"), None, "sp", "sec"),
        P(("grp", "mb"), None, "sp", None),
        P(("grp", "mb"), None, "sp", None),
        P("sp", None),
        P(),
        P(),
        P(),
        P(),
        P(),
    )
    return jax.shard_map(
        shards,
        mesh=mesh,
        in_specs=placed,
        out_specs=(P(("grp", "mb"), None, "sp", "sec"), P(("grp", "mb"), None, "sp", None)),
        check_vma=False,
    )
```

```python
import functools

import jax
import jax.numpy as jnp
from jax import lax
from jax.experimental import pallas as pl
from jax.experimental.pallas import tpu as pltpu
from jax.sharding import PartitionSpec as P

STEPS = 2
SEA_DILATIONS = (1, 1)
AIR_DILATIONS = (1, 2, 4)
LANES = 128
MESH = pl.DeviceIdType.MESH
F32 = jnp.float32
BF16 = jnp.bfloat16


def round_up(value, unit):
    return -(-value // unit) * unit


def rounded(value):
    return value.astype(BF16).astype(F32)


def gelu(v):
    return 0.5 * v * (1.0 + jnp.tanh(0.7978845608028654 * (v + 0.044715 * (v * v * v))))


def kernel(
    dims,
    atm_ref, sea_ref, flux_ref, mask_ref, h_air1, h_air2, h_air3, h_sea1, h_sea2,
    air_out, sea_out,
    got_atm, got_sea, got_flux, got_mask, got_edge, edge_src,
    atm_f, sea_f, flux_f, mask_f, edge_p, hidden_a, hidden_b,
    stage, stage_sea, fin_air_src, fin_air, fin_sea_src, fin_sea, product,
    r_air1, r_air2, r_air3, r_sea1, r_sea2, w_air1, w_air2, w_air3, w_sea1, w_sea2,
    atm_send, atm_recv, near_send, near_recv, edge_send, edge_recv,
    fin_air_send, fin_air_recv, fin_sea_send, fin_sea_recv, weight_sem,
):
    sp, sections, members, rows, fields, surface, cols, window, home, hidden = dims
    bands = sections - 1
    total = window * rows
    own = home * rows
    me = lax.axis_index("sp")
    sec = lax.axis_index("sec")
    member = lax.rem(sec, members)
    base = sec - member
    in_band = sec < bands

    weight_copies = [
        pltpu.make_async_copy(src, dst, weight_sem.at[k])
        for k, (src, dst) in enumerate((
            (h_sea1, r_sea1), (h_sea2, r_sea2), (h_air1, r_air1), (h_air3, r_air3),
            (h_air2, r_air2),
        ))
    ]
    for copy in weight_copies:
        copy.start()

    def target_row(slot):
        return lax.rem(me - slot + home + 2 * sp, sp)

    lane = lax.broadcasted_iota(jnp.int32, (fields, LANES), 1)

    @pl.when(sec == bands)
    def _():
        for m in range(members):
            stage[0] = atm_ref[m].astype(F32)
            tile = jnp.zeros((fields, LANES), F32)
            for r in range(rows):
                line = stage[0, pl.ds(r, fields, stride=rows), :]
                line = line if r == 0 else pltpu.roll(line, r, 1)
                tile = jnp.where(lane == r, line, tile)
            edge_src[m] = jnp.concatenate(
                [tile, jnp.zeros((surface, LANES), F32)], axis=0
            ).astype(BF16)
        got_edge[home] = edge_src[member]

    @pl.when(in_band)
    def _():
        got_atm[home, jnp.minimum(sec, bands - 1)] = atm_ref[member]

    got_sea[home] = sea_ref[member]
    got_flux[home] = flux_ref[member]
    got_mask[home] = mask_ref[...]

    barrier = pltpu.get_barrier_semaphore()
    for slot in range(window):
        for to in range(sections):
            far = slot != home

            def greet(slot=slot, to=to):
                pl.semaphore_signal(
                    barrier, inc=1, device_id={"sp": target_row(slot), "sec": to},
                    device_id_type=MESH,
                )

            if far:
                greet()
            else:
                pl.when(sec != to)(greet)
    pl.semaphore_wait(barrier, window * sections - 1)

    def near_copies(slot):
        place = {"sp": target_row(slot), "sec": sec}
        pairs = (
            (sea_ref.at[member], got_sea.at[slot]),
            (flux_ref.at[member], got_flux.at[slot]),
            (mask_ref, got_mask.at[slot]),
        )
        return [
            pltpu.make_async_remote_copy(
                src_ref=src, dst_ref=dst,
                send_sem=near_send.at[slot, k], recv_sem=near_recv.at[slot, k],
                device_id=place, device_id_type=MESH,
            )
            for k, (src, dst) in enumerate(pairs)
        ]

    def atm_copy(slot, to, band):
        return pltpu.make_async_remote_copy(
            src_ref=atm_ref.at[to % members], dst_ref=got_atm.at[slot, band],
            send_sem=atm_send.at[slot, to], recv_sem=atm_recv.at[slot, band],
            device_id={"sp": target_row(slot), "sec": to}, device_id_type=MESH,
        )

    def edge_copy(slot, to):
        return pltpu.make_async_remote_copy(
            src_ref=edge_src.at[to % members], dst_ref=got_edge.at[slot],
            send_sem=edge_send.at[slot, to], recv_sem=edge_recv.at[slot],
            device_id={"sp": target_row(slot), "sec": to}, device_id_type=MESH,
        )

    slots = sorted(range(window), key=lambda slot: -abs(slot - home))
    for slot in slots:
        if slot != home:
            for copy in near_copies(slot):
                copy.start()

    def each_target(act):
        for slot in slots:
            for to in range(sections):
                if slot == home:
                    pl.when(sec != to)(functools.partial(act, slot, to))
                else:
                    act(slot, to)

    @pl.when(in_band)
    def _():
        band = jnp.minimum(sec, bands - 1)
        each_target(lambda slot, to: atm_copy(slot, to, band).start())

    @pl.when(sec == bands)
    def _():
        each_target(lambda slot, to: edge_copy(slot, to).start())

    column = lax.broadcasted_iota(jnp.int32, (1, cols), 1)
    tile_rows = max(1, 512 // cols)

    def span(margin):
        count = round_up(rows + 2 * margin, tile_rows)
        if count >= total:
            return 0, total
        return own - margin, count

    def conv(load, weight_ref, outs, dilation, margin, emit):
        start, count = span(margin)
        chunks = count // tile_rows

        def multiply(i):
            first = start + i * tile_rows + 2 * total
            pieces = []
            for t in range(tile_rows):
                taps = [load(lax.rem(first + t + (a - 1) * dilation, total)) for a in range(3)]
                pieces.append(jnp.concatenate([
                    part for level in zip(*taps) for part in level
                ], axis=0))
            block = pieces[0] if tile_rows == 1 else jnp.concatenate(pieces, axis=1)
            product[:3 * outs] = jnp.dot(
                weight_ref[:, :block.shape[0]], block, preferred_element_type=F32
            )

        def finish(i):
            first = start + i * tile_rows + 2 * total
            for t in range(tile_rows):
                part = slice(t * cols, (t + 1) * cols)
                left = pltpu.roll(product[:outs, part], dilation, 1)
                right = pltpu.roll(product[2 * outs:3 * outs, part], cols - dilation, 1)
                value = product[outs:2 * outs, part]
                value = value + jnp.where(column >= dilation, left, 0.0)
                value = value + jnp.where(column < cols - dilation, right, 0.0)
                emit(lax.rem(first + t, total), value)

        def step(i, carry):
            finish(i)
            multiply(i + 1)
            return carry

        multiply(0)
        lax.fori_loop(0, chunks - 1, step, 0)
        finish(chunks - 1)

    def load_sea(r):
        return [jnp.concatenate([sea_f[r], flux_f[r]], axis=0).astype(BF16)]

    def load_air(r):
        return [jnp.concatenate([atm_f[r], sea_f[r]], axis=0).astype(BF16)]

    def load_hidden(ref):
        return lambda r: [ref[r, at:min(at + LANES, ref.shape[1])]
                          for at in range(0, ref.shape[1], LANES)]

    def keep(ref):
        def emit(r, value):
            made = gelu(value)
            spare = jnp.zeros((ref.shape[1] - hidden, cols), F32)
            ref[r] = jnp.concatenate([made, spare], axis=0).astype(BF16)
        return emit

    def emit_sea(r, value):
        sea_f[r] = rounded(sea_f[r] + mask_f[r] * value)

    last_lane = lax.broadcasted_iota(jnp.int32, (hidden, LANES), 1) == LANES - 1

    def emit_air1(r, value):
        rim = jnp.where(last_lane, pltpu.roll(edge_p[...], LANES - 1 - r, 1), 0.0)
        if cols > LANES:
            rim = jnp.concatenate([jnp.zeros((hidden, cols - LANES), F32), rim], axis=1)
        keep(hidden_a)(r, value + rim)

    def emit_air3(r, value):
        atm_f[r] = rounded(atm_f[r] + value[:fields])
        flux_f[r] = rounded(value[fields:])

    def lay_out(raw, laid, depth, outs, turned):
        at = 0
        for low in range(0, depth, LANES):
            high = min(low + LANES, depth)
            panels = [[a] for a in range(3)] if high - low == LANES else [[0, 1, 2]]
            for taps in panels:
                columns = []
                for b in range(3):
                    parts = []
                    for a in taps:
                        if turned:
                            part = raw[3 * a + b].astype(F32)[:, low:high]
                        else:
                            part = raw[3 * a + b, low:high, :].astype(F32)
                        spare = round_up(high - low, 16) - (high - low)
                        if spare:
                            shape = (outs, spare) if turned else (spare, outs)
                            part = jnp.concatenate(
                                [part, jnp.zeros(shape, F32)], axis=1 if turned else 0
                            )
                        parts.append(part)
                    axis = 1 if turned else 0
                    width = sum(part.shape[axis] for part in parts)
                    if width < LANES:
                        shape = (outs, LANES - width) if turned else (LANES - width, outs)
                        parts.append(jnp.zeros(shape, F32))
                    block = parts[0] if len(parts) == 1 else jnp.concatenate(parts, axis=axis)
                    columns.append(block if turned else block.T)
                laid[:, at:at + LANES] = jnp.concatenate(columns, axis=0).astype(BF16)
                at += LANES

    for copy in weight_copies:
        copy.wait()
    lay_out(r_sea1, w_sea1, 2 * surface, hidden, False)
    lay_out(r_sea2, w_sea2, hidden, surface, True)
    lay_out(r_air1, w_air1, fields + surface, hidden, False)
    lay_out(r_air3, w_air3, hidden, fields + surface, True)
    lay_out(r_air2, w_air2, hidden, hidden, False)

    for slot in range(window):
        if slot != home:
            for copy in near_copies(slot):
                copy.wait_recv()
        for k, (got, state) in enumerate(((got_sea, sea_f), (got_flux, flux_f))):
            for band in range(bands):
                part = slice(band * LANES, (band + 1) * LANES)
                stage_sea[band] = got[slot, :, part].astype(F32)
                for r in range(rows):
                    state[slot * rows + r, :, part] = stage_sea[
                        band, pl.ds(r, surface, stride=rows), :
                    ]
        weight = got_mask[slot].astype(F32)
        for r in range(rows):
            mask_f[slot * rows + r] = jnp.broadcast_to(weight[r:r + 1], (surface, cols))

    def take_atmosphere():
        for slot in range(window):
            for band in range(bands):
                if slot == home:
                    pl.when(sec != band)(lambda: atm_copy(slot, 0, band).wait_recv())
                else:
                    atm_copy(slot, 0, band).wait_recv()
                stage[band] = got_atm[slot, band].astype(F32)
                for r in range(rows):
                    atm_f[slot * rows + r, :, band * LANES:(band + 1) * LANES] = stage[
                        band, pl.ds(r, fields, stride=rows), :
                    ]
            if slot == home:
                pl.when(sec != bands)(lambda: edge_copy(slot, 0).wait_recv())
            else:
                edge_copy(slot, 0).wait_recv()
        place = lax.broadcasted_iota(jnp.int32, (fields + surface, LANES), 1)
        edge = jnp.zeros((fields + surface, LANES), F32)
        for slot in range(window):
            part = got_edge[slot].astype(F32)
            edge = edge + (part if slot == 0 else pltpu.roll(part, slot * rows, 1))
        above = jnp.where(
            place == 0, pltpu.roll(edge, LANES - (total - 1), 1), pltpu.roll(edge, 1, 1)
        )
        below = jnp.where(
            place == total - 1, pltpu.roll(edge, total - 1, 1), pltpu.roll(edge, LANES - 1, 1)
        )
        three = jnp.concatenate([above, edge, below], axis=0).astype(BF16)
        edge_p[...] = jnp.dot(
            w_air1[2 * hidden:3 * hidden, :three.shape[0]], three, preferred_element_type=F32
        )

    halo = sum(SEA_DILATIONS) + sum(AIR_DILATIONS)
    for step in range(STEPS):
        after = (STEPS - 1 - step) * halo
        air = sum(AIR_DILATIONS)
        conv(load_sea, w_sea1, hidden, 1, after + air + 1, keep(hidden_a))
        conv(load_hidden(hidden_a), w_sea2, surface, 1, after + air, emit_sea)
        if step == STEPS - 1:
            for band in range(bands):
                part = slice(band * LANES, (band + 1) * LANES)
                for r in range(rows):
                    stage_sea[band, pl.ds(r, surface, stride=rows), :] = sea_f[own + r, :, part]
                fin_sea_src[:, part] = stage_sea[band].astype(BF16)
            sea_copies = []
            for k in range(1, members):
                to = lax.rem(member + k, members)
                sea_copies.append(pltpu.make_async_remote_copy(
                    src_ref=fin_sea_src, dst_ref=fin_sea.at[member],
                    send_sem=fin_sea_send.at[k], recv_sem=fin_sea_recv.at[member],
                    device_id={"sec": base + to}, device_id_type=MESH,
                ))
                sea_copies[-1].start()
        if step == 0:
            take_atmosphere()
        conv(load_air, w_air1, hidden, 1, after + 6, emit_air1)
        conv(load_hidden(hidden_a), w_air2, hidden, 2, after + 4, keep(hidden_b))
        conv(load_hidden(hidden_b), w_air3, fields + surface, 4, after, emit_air3)

    for band in range(bands):
        for r in range(rows):
            stage[band, pl.ds(r, fields, stride=rows), :] = atm_f[
                own + r, :, band * LANES:(band + 1) * LANES
            ]
        fin_air_src[band] = stage[band].astype(BF16)

    def air_copy(k, landing):
        to = base + lax.rem(member + k, members)
        return to, pltpu.make_async_remote_copy(
            src_ref=fin_air_src.at[jnp.minimum(to, bands - 1)], dst_ref=fin_air.at[landing],
            send_sem=fin_air_send.at[k], recv_sem=fin_air_recv.at[landing],
            device_id={"sec": to}, device_id_type=MESH,
        )

    for k in range(1, members):
        to, copy = air_copy(k, member)
        pl.when(to < bands)(copy.start)

    sea_out[member] = fin_sea_src[...]
    for k in range(1, members):
        origin = lax.rem(member + k, members)
        pltpu.make_async_remote_copy(
            src_ref=fin_sea_src, dst_ref=fin_sea.at[origin],
            send_sem=fin_sea_send.at[k], recv_sem=fin_sea_recv.at[origin],
            device_id={"sec": base + origin}, device_id_type=MESH,
        ).wait_recv()
        sea_out[origin] = fin_sea[origin]

    @pl.when(sec == bands)
    def _():
        air_out[...] = atm_ref[...]

    @pl.when(in_band)
    def _():
        air_out[member] = fin_air_src[jnp.minimum(sec, bands - 1)]
        for k in range(1, members):
            origin = lax.rem(member + k, members)
            air_copy(k, origin)[1].wait_recv()
            air_out[origin] = fin_air[origin]

    for copy in sea_copies:
        copy.wait_send()
    for k in range(1, members):
        to, copy = air_copy(k, member)
        pl.when(to < bands)(copy.wait_send)
    for slot in slots:
        if slot != home:
            for copy in near_copies(slot):
                copy.wait_send()

    @pl.when(in_band)
    def _():
        band = jnp.minimum(sec, bands - 1)
        each_target(lambda slot, to: atm_copy(slot, to, band).wait_send())

    @pl.when(sec == bands)
    def _():
        each_target(lambda slot, to: edge_copy(slot, to).wait_send())


def taps_first(weight, turned=False):
    weight = weight.reshape((-1,) + weight.shape[2:])
    return weight.transpose(0, 2, 1) if turned else weight


def shards(
    atmosphere, ocean_state, fluxes, sea_mask, air_entry, air_middle, air_exit, sea_entry, sea_exit
):
    sp = lax.axis_size("sp")
    sections = lax.axis_size("sec")
    bands = sections - 1
    members, fields, rows, band_cols = atmosphere.shape
    surface, cols = ocean_state.shape[1], ocean_state.shape[3]
    hidden = air_entry.shape[3]
    reach = STEPS * (sum(SEA_DILATIONS) + sum(AIR_DILATIONS))
    window = min(sp, 2 * (-(-reach // rows)) + 1)
    home = (window - 1) // 2
    total = window * rows
    depth = round_up(hidden, 16)
    assert band_cols == LANES and cols == bands * band_cols
    assert sections % members == 0 and total <= LANES and surface == fluxes.shape[1]
    dims = (sp, sections, members, rows, fields, surface, cols, window, home, hidden)
    dma = pltpu.SemaphoreType.DMA
    flat = fields * rows
    flat_sea = surface * rows
    raw = (
        taps_first(air_entry), taps_first(air_middle), taps_first(air_exit, True),
        taps_first(sea_entry), taps_first(sea_exit, True),
    )
    air_depth = LANES * (3 * (hidden // LANES) + 1)
    tile_cols = max(1, 512 // cols) * cols
    air, sea = pl.pallas_call(
        functools.partial(kernel, dims),
        out_shape=(
            jax.ShapeDtypeStruct((members, flat, band_cols), BF16),
            jax.ShapeDtypeStruct((members, flat_sea, cols), BF16),
        ),
        in_specs=[pl.BlockSpec(memory_space=pltpu.VMEM)] * 4
        + [pl.BlockSpec(memory_space=pl.ANY)] * 5,
        out_specs=(pl.BlockSpec(memory_space=pltpu.VMEM),) * 2,
        scratch_shapes=[
            pltpu.VMEM((window, bands, flat, LANES), BF16),
            pltpu.VMEM((window, flat_sea, cols), BF16),
            pltpu.VMEM((window, flat_sea, cols), BF16),
            pltpu.VMEM((window, rows, cols), jnp.int32),
            pltpu.VMEM((window, fields + surface, LANES), BF16),
            pltpu.VMEM((members, fields + surface, LANES), BF16),
            pltpu.VMEM((total, fields, cols), F32),
            pltpu.VMEM((total, surface, cols), F32),
            pltpu.VMEM((total, surface, cols), F32),
            pltpu.VMEM((total, surface, cols), F32),
            pltpu.VMEM((hidden, LANES), F32),
            pltpu.VMEM((total, depth, cols), BF16),
            pltpu.VMEM((total, depth, cols), BF16),
            pltpu.VMEM((bands, flat, LANES), F32),
            pltpu.VMEM((bands, flat_sea, LANES), F32),
            pltpu.VMEM((bands, flat, LANES), BF16),
            pltpu.VMEM((members, flat, LANES), BF16),
            pltpu.VMEM((flat_sea, cols), BF16),
            pltpu.VMEM((members, flat_sea, cols), BF16),
            pltpu.VMEM((3 * hidden, tile_cols), F32),
            *[pltpu.VMEM(weight.shape, BF16) for weight in raw],
            pltpu.VMEM((3 * hidden, LANES), BF16),
            pltpu.VMEM((3 * hidden, air_depth), BF16),
            pltpu.VMEM((3 * (fields + surface), air_depth), BF16),
            pltpu.VMEM((3 * hidden, LANES), BF16),
            pltpu.VMEM((3 * surface, air_depth), BF16),
            dma((window, sections)),
            dma((window, bands)),
            dma((window, 3)),
            dma((window, 3)),
            dma((window, sections)),
            dma((window,)),
            dma((members,)),
            dma((members,)),
            dma((members,)),
            dma((members,)),
            dma((len(raw),)),
        ],
        compiler_params=pltpu.CompilerParams(
            collective_id=0, has_side_effects=True, vmem_limit_bytes=63 * 1024 * 1024
        ),
    )(
        atmosphere.reshape(members, flat, band_cols),
        ocean_state.reshape(members, flat_sea, cols),
        fluxes.reshape(members, flat_sea, cols),
        sea_mask,
        *raw,
    )
    return air.reshape(atmosphere.shape), sea.reshape(ocean_state.shape)


def solution(mesh):
    placed = (
        P(("grp", "mb"), None, "sp", "sec"),
        P(("grp", "mb"), None, "sp", None),
        P(("grp", "mb"), None, "sp", None),
        P("sp", None),
        P(),
        P(),
        P(),
        P(),
        P(),
    )
    return jax.shard_map(
        shards,
        mesh=mesh,
        in_specs=placed,
        out_specs=(P(("grp", "mb"), None, "sp", "sec"), P(("grp", "mb"), None, "sp", None)),
        check_vma=False,
    )
```

```python
import functools

import jax
import jax.numpy as jnp
from jax import lax
from jax.experimental import pallas as pl
from jax.experimental.pallas import tpu as pltpu
from jax.sharding import PartitionSpec as P

STEPS = 2
SEA_DILATIONS = (1, 1)
AIR_DILATIONS = (1, 2, 4)
LANES = 128
TILE_COLS = 1024
MESH = pl.DeviceIdType.MESH
F32 = jnp.float32
BF16 = jnp.bfloat16


def round_up(value, unit):
    return -(-value // unit) * unit


def rounded(value):
    return value.astype(BF16).astype(F32)


def gelu(v):
    return 0.5 * v * (1.0 + jnp.tanh(0.7978845608028654 * (v + 0.044715 * (v * v * v))))


def kernel(
    dims,
    atm_ref, sea_ref, flux_ref, mask_ref, h_air1, h_air2, h_air3, h_sea1, h_sea2,
    air_out, sea_out,
    got_atm, got_sea, got_flux, got_mask, got_edge, edge_src,
    atm_f, sea_f, flux_f, mask_f, edge_f, wide_sea, wide_air, hidden_a, hidden_b,
    stage, stage_sea, fin_air_src, fin_air, fin_sea_src, fin_sea, product,
    r_air1, r_air2, r_air3, r_sea1, r_sea2, w_air1, w_air2, w_air3, w_sea1, w_sea2,
    atm_send, atm_recv, near_send, near_recv, edge_send, edge_recv,
    fin_air_send, fin_air_recv, fin_sea_send, fin_sea_recv, weight_sem,
):
    sp, sections, members, rows, fields, surface, cols, window, home, hidden = dims
    bands = sections - 1
    total = window * rows
    own = home * rows
    me = lax.axis_index("sp")
    sec = lax.axis_index("sec")
    member = lax.rem(sec, members)
    base = sec - member
    in_band = sec < bands

    weight_copies = [
        pltpu.make_async_copy(src, dst, weight_sem.at[k])
        for k, (src, dst) in enumerate((
            (h_sea1, r_sea1), (h_sea2, r_sea2), (h_air1, r_air1), (h_air3, r_air3),
            (h_air2, r_air2),
        ))
    ]
    for copy in weight_copies:
        copy.start()

    def target_row(slot):
        return lax.rem(me - slot + home + 2 * sp, sp)

    lane = lax.broadcasted_iota(jnp.int32, (fields, LANES), 1)

    @pl.when(sec == bands)
    def _():
        for m in range(members):
            stage[0] = atm_ref[m].astype(F32)
            tile = jnp.zeros((fields, LANES), F32)
            for r in range(rows):
                line = stage[0, pl.ds(r, fields, stride=rows), :]
                line = line if r == 0 else pltpu.roll(line, r, 1)
                tile = jnp.where(lane == r, line, tile)
            edge_src[m] = jnp.concatenate(
                [tile, jnp.zeros((surface, LANES), F32)], axis=0
            ).astype(BF16)
        got_edge[home] = edge_src[member]

    @pl.when(in_band)
    def _():
        got_atm[home, jnp.minimum(sec, bands - 1)] = atm_ref[member]

    got_sea[home] = sea_ref[member]
    got_flux[home] = flux_ref[member]
    got_mask[home] = mask_ref[...]

    barrier = pltpu.get_barrier_semaphore()
    for slot in range(window):
        for to in range(sections):
            far = slot != home

            def greet(slot=slot, to=to):
                pl.semaphore_signal(
                    barrier, inc=1, device_id={"sp": target_row(slot), "sec": to},
                    device_id_type=MESH,
                )

            if far:
                greet()
            else:
                pl.when(sec != to)(greet)
    def lay_out(raw, laid, depth, outs, turned):
        at = 0
        for low in range(0, depth, LANES):
            high = min(low + LANES, depth)
            panels = [[a] for a in range(3)] if high - low == LANES else [[0, 1, 2]]
            for taps in panels:
                columns = []
                for b in range(3):
                    parts = []
                    for a in taps:
                        if turned:
                            part = raw[3 * a + b].astype(F32)[:, low:high]
                        else:
                            part = raw[3 * a + b, low:high, :].astype(F32)
                        spare = round_up(high - low, 16) - (high - low)
                        if spare:
                            shape = (outs, spare) if turned else (spare, outs)
                            part = jnp.concatenate(
                                [part, jnp.zeros(shape, F32)], axis=1 if turned else 0
                            )
                        parts.append(part)
                    axis = 1 if turned else 0
                    width = sum(part.shape[axis] for part in parts)
                    if width < LANES:
                        shape = (outs, LANES - width) if turned else (LANES - width, outs)
                        parts.append(jnp.zeros(shape, F32))
                    block = parts[0] if len(parts) == 1 else jnp.concatenate(parts, axis=axis)
                    columns.append(block if turned else block.T)
                laid[:, at:at + LANES] = jnp.concatenate(columns, axis=0).astype(BF16)
                at += LANES

    def turn(raw, laid):
        depth = raw.shape[0]
        for low in range(0, depth, LANES):
            part = raw[low:min(low + LANES, depth), :].astype(F32)
            if part.shape[0] < LANES:
                spare = jnp.zeros((LANES - part.shape[0], part.shape[1]), F32)
                part = jnp.concatenate([part, spare], axis=0)
            laid[:, low:low + LANES] = part.T.astype(BF16)

    for copy in weight_copies:
        copy.wait()
    turn(r_sea1, w_sea1)
    lay_out(r_air2, w_air2, hidden, hidden, False)
    pl.semaphore_wait(barrier, window * sections - 1)

    def near_copies(slot):
        place = {"sp": target_row(slot), "sec": sec}
        pairs = (
            (sea_ref.at[member], got_sea.at[slot]),
            (flux_ref.at[member], got_flux.at[slot]),
            (mask_ref, got_mask.at[slot]),
        )
        return [
            pltpu.make_async_remote_copy(
                src_ref=src, dst_ref=dst,
                send_sem=near_send.at[slot, k], recv_sem=near_recv.at[slot, k],
                device_id=place, device_id_type=MESH,
            )
            for k, (src, dst) in enumerate(pairs)
        ]

    def atm_copy(slot, to, band):
        return pltpu.make_async_remote_copy(
            src_ref=atm_ref.at[to % members], dst_ref=got_atm.at[slot, band],
            send_sem=atm_send.at[slot, to], recv_sem=atm_recv.at[slot, band],
            device_id={"sp": target_row(slot), "sec": to}, device_id_type=MESH,
        )

    def edge_copy(slot, to):
        return pltpu.make_async_remote_copy(
            src_ref=edge_src.at[to % members], dst_ref=got_edge.at[slot],
            send_sem=edge_send.at[slot, to], recv_sem=edge_recv.at[slot],
            device_id={"sp": target_row(slot), "sec": to}, device_id_type=MESH,
        )

    slots = sorted(range(window), key=lambda slot: -abs(slot - home))
    for slot in slots:
        if slot != home:
            for copy in near_copies(slot):
                copy.start()

    def each_target(act):
        for slot in slots:
            for to in range(sections):
                if slot == home:
                    pl.when(sec != to)(functools.partial(act, slot, to))
                else:
                    act(slot, to)

    @pl.when(in_band)
    def _():
        band = jnp.minimum(sec, bands - 1)
        each_target(lambda slot, to: atm_copy(slot, to, band).start())

    @pl.when(sec == bands)
    def _():
        each_target(lambda slot, to: edge_copy(slot, to).start())

    column = lax.broadcasted_iota(jnp.int32, (1, cols), 1)
    tile_rows = max(1, TILE_COLS // cols)

    def span(margin):
        count = round_up(rows + 2 * margin, tile_rows)
        if count >= total:
            return 0, total
        return own - margin, count

    def conv(load, weight_ref, outs, dilation, margin, emit):
        start, count = span(margin)
        chunks = count // tile_rows

        def multiply(i):
            first = start + i * tile_rows + 2 * total
            pieces = []
            for t in range(tile_rows):
                taps = [load(lax.rem(first + t + (a - 1) * dilation, total)) for a in range(3)]
                pieces.append(jnp.concatenate([
                    part for level in zip(*taps) for part in level
                ], axis=0))
            block = pieces[0] if tile_rows == 1 else jnp.concatenate(pieces, axis=1)
            product[:weight_ref.shape[0]] = jnp.dot(
                weight_ref[:, :block.shape[0]], block, preferred_element_type=F32
            )

        def finish(i):
            first = start + i * tile_rows + 2 * total
            for t in range(tile_rows):
                part = slice(t * cols, (t + 1) * cols)
                if weight_ref.shape[0] == outs:
                    emit(lax.rem(first + t, total), product[:outs, part])
                    continue
                left = pltpu.roll(product[:outs, part], dilation, 1)
                right = pltpu.roll(product[2 * outs:3 * outs, part], cols - dilation, 1)
                value = product[outs:2 * outs, part]
                value = value + jnp.where(column >= dilation, left, 0.0)
                value = value + jnp.where(column < cols - dilation, right, 0.0)
                emit(lax.rem(first + t, total), value)

        def step(i, carry):
            finish(i)
            multiply(i + 1)
            return carry

        multiply(0)
        lax.fori_loop(0, chunks - 1, step, 0)
        finish(chunks - 1)

    last_lane = lax.broadcasted_iota(jnp.int32, (1, LANES), 1) == LANES - 1

    def widen(top, bottom, wide, rim=None):
        def step(i, carry):
            for t in range(rows):
                r = i * rows + t
                here = jnp.concatenate([top[r], bottom[r]], axis=0)
                left = jnp.where(column >= 1, pltpu.roll(here, 1, 1), 0.0)
                right = jnp.where(column < cols - 1, pltpu.roll(here, cols - 1, 1), 0.0)
                if rim is not None:
                    beside = jnp.where(last_lane, pltpu.roll(rim[...], LANES - 1 - r, 1), 0.0)
                    if cols > LANES:
                        blank = jnp.zeros((here.shape[0], cols - LANES), F32)
                        beside = jnp.concatenate([blank, beside], axis=1)
                    right = right + beside
                wide[r] = jnp.concatenate([left, here, right], axis=0).astype(BF16)
            return carry

        lax.fori_loop(0, window, step, 0)

    def load_hidden(ref):
        return lambda r: [ref[r, at:min(at + LANES, ref.shape[1])]
                          for at in range(0, ref.shape[1], LANES)]

    def keep(ref):
        def emit(r, value):
            made = gelu(value)
            spare = jnp.zeros((ref.shape[1] - hidden, cols), F32)
            ref[r] = jnp.concatenate([made, spare], axis=0).astype(BF16)
        return emit

    def emit_sea(r, value):
        sea_f[r] = rounded(sea_f[r] + mask_f[r] * value)

    def emit_air3(r, value):
        atm_f[r] = rounded(atm_f[r] + value[:fields])
        flux_f[r] = rounded(value[fields:])

    lay_out(r_sea2, w_sea2, hidden, surface, True)
    turn(r_air1, w_air1)
    lay_out(r_air3, w_air3, hidden, fields + surface, True)

    for slot in range(window):
        if slot != home:
            for copy in near_copies(slot):
                copy.wait_recv()
        for k, (got, state) in enumerate(((got_sea, sea_f), (got_flux, flux_f))):
            for band in range(bands):
                part = slice(band * LANES, (band + 1) * LANES)
                stage_sea[band] = got[slot, :, part].astype(F32)
                for r in range(rows):
                    state[slot * rows + r, :, part] = stage_sea[
                        band, pl.ds(r, surface, stride=rows), :
                    ]
        weight = got_mask[slot].astype(F32)
        for r in range(rows):
            mask_f[slot * rows + r] = jnp.broadcast_to(weight[r:r + 1], (surface, cols))

    def take_atmosphere():
        for slot in range(window):
            for band in range(bands):
                if slot == home:
                    pl.when(sec != band)(lambda: atm_copy(slot, 0, band).wait_recv())
                else:
                    atm_copy(slot, 0, band).wait_recv()
                stage[band] = got_atm[slot, band].astype(F32)
                for r in range(rows):
                    atm_f[slot * rows + r, :, band * LANES:(band + 1) * LANES] = stage[
                        band, pl.ds(r, fields, stride=rows), :
                    ]
            if slot == home:
                pl.when(sec != bands)(lambda: edge_copy(slot, 0).wait_recv())
            else:
                edge_copy(slot, 0).wait_recv()
        edge = jnp.zeros((fields + surface, LANES), F32)
        for slot in range(window):
            part = got_edge[slot].astype(F32)
            edge = edge + (part if slot == 0 else pltpu.roll(part, slot * rows, 1))
        edge_f[...] = edge

    halo = sum(SEA_DILATIONS) + sum(AIR_DILATIONS)
    for step in range(STEPS):
        after = (STEPS - 1 - step) * halo
        air = sum(AIR_DILATIONS)
        widen(sea_f, flux_f, wide_sea)
        conv(lambda r: [wide_sea[r]], w_sea1, hidden, 1, after + air + 1, keep(hidden_a))
        conv(load_hidden(hidden_a), w_sea2, surface, 1, after + air, emit_sea)
        if step == STEPS - 1:
            for band in range(bands):
                part = slice(band * LANES, (band + 1) * LANES)
                for r in range(rows):
                    stage_sea[band, pl.ds(r, surface, stride=rows), :] = sea_f[own + r, :, part]
                fin_sea_src[:, part] = stage_sea[band].astype(BF16)
            sea_copies = []
            for k in range(1, members):
                to = lax.rem(member + k, members)
                sea_copies.append(pltpu.make_async_remote_copy(
                    src_ref=fin_sea_src, dst_ref=fin_sea.at[member],
                    send_sem=fin_sea_send.at[k], recv_sem=fin_sea_recv.at[member],
                    device_id={"sec": base + to}, device_id_type=MESH,
                ))
                sea_copies[-1].start()
        if step == 0:
            take_atmosphere()
        widen(atm_f, sea_f, wide_air, edge_f)
        conv(lambda r: [wide_air[r]], w_air1, hidden, 1, after + 6, keep(hidden_a))
        conv(load_hidden(hidden_a), w_air2, hidden, 2, after + 4, keep(hidden_b))
        conv(load_hidden(hidden_b), w_air3, fields + surface, 4, after, emit_air3)

    for band in range(bands):
        for r in range(rows):
            stage[band, pl.ds(r, fields, stride=rows), :] = atm_f[
                own + r, :, band * LANES:(band + 1) * LANES
            ]
        fin_air_src[band] = stage[band].astype(BF16)

    def air_copy(k, landing):
        to = base + lax.rem(member + k, members)
        return to, pltpu.make_async_remote_copy(
            src_ref=fin_air_src.at[jnp.minimum(to, bands - 1)], dst_ref=fin_air.at[landing],
            send_sem=fin_air_send.at[k], recv_sem=fin_air_recv.at[landing],
            device_id={"sec": to}, device_id_type=MESH,
        )

    for k in range(1, members):
        to, copy = air_copy(k, member)
        pl.when(to < bands)(copy.start)

    sea_out[member] = fin_sea_src[...]
    for k in range(1, members):
        origin = lax.rem(member + k, members)
        pltpu.make_async_remote_copy(
            src_ref=fin_sea_src, dst_ref=fin_sea.at[origin],
            send_sem=fin_sea_send.at[k], recv_sem=fin_sea_recv.at[origin],
            device_id={"sec": base + origin}, device_id_type=MESH,
        ).wait_recv()
        sea_out[origin] = fin_sea[origin]

    @pl.when(sec == bands)
    def _():
        air_out[...] = atm_ref[...]

    @pl.when(in_band)
    def _():
        air_out[member] = fin_air_src[jnp.minimum(sec, bands - 1)]
        for k in range(1, members):
            origin = lax.rem(member + k, members)
            air_copy(k, origin)[1].wait_recv()
            air_out[origin] = fin_air[origin]

    for copy in sea_copies:
        copy.wait_send()
    for k in range(1, members):
        to, copy = air_copy(k, member)
        pl.when(to < bands)(copy.wait_send)
    for slot in slots:
        if slot != home:
            for copy in near_copies(slot):
                copy.wait_send()

    @pl.when(in_band)
    def _():
        band = jnp.minimum(sec, bands - 1)
        each_target(lambda slot, to: atm_copy(slot, to, band).wait_send())

    @pl.when(sec == bands)
    def _():
        each_target(lambda slot, to: edge_copy(slot, to).wait_send())


def taps_first(weight):
    return weight.reshape((-1,) + weight.shape[2:])


def shards(
    atmosphere, ocean_state, fluxes, sea_mask, air_entry, air_middle, air_exit, sea_entry, sea_exit
):
    sp = lax.axis_size("sp")
    sections = lax.axis_size("sec")
    bands = sections - 1
    members, fields, rows, band_cols = atmosphere.shape
    surface, cols = ocean_state.shape[1], ocean_state.shape[3]
    hidden = air_entry.shape[3]
    reach = STEPS * (sum(SEA_DILATIONS) + sum(AIR_DILATIONS))
    window = min(sp, 2 * (-(-reach // rows)) + 1)
    home = (window - 1) // 2
    total = window * rows
    depth = round_up(hidden, 16)
    assert band_cols == LANES and cols == bands * band_cols
    assert sections % members == 0 and total <= LANES and surface == fluxes.shape[1]
    dims = (sp, sections, members, rows, fields, surface, cols, window, home, hidden)
    dma = pltpu.SemaphoreType.DMA
    flat = fields * rows
    flat_sea = surface * rows
    raw = (
        air_entry.reshape(-1, hidden), taps_first(air_middle),
        taps_first(air_exit).transpose(0, 2, 1),
        sea_entry.reshape(-1, hidden), taps_first(sea_exit).transpose(0, 2, 1),
    )
    air_depth = LANES * (3 * (hidden // LANES) + 1)
    tile_cols = max(1, TILE_COLS // cols) * cols
    air, sea = pl.pallas_call(
        functools.partial(kernel, dims),
        out_shape=(
            jax.ShapeDtypeStruct((members, flat, band_cols), BF16),
            jax.ShapeDtypeStruct((members, flat_sea, cols), BF16),
        ),
        in_specs=[pl.BlockSpec(memory_space=pltpu.VMEM)] * 4
        + [pl.BlockSpec(memory_space=pl.ANY)] * 5,
        out_specs=(pl.BlockSpec(memory_space=pltpu.VMEM),) * 2,
        scratch_shapes=[
            pltpu.VMEM((window, bands, flat, LANES), BF16),
            pltpu.VMEM((window, flat_sea, cols), BF16),
            pltpu.VMEM((window, flat_sea, cols), BF16),
            pltpu.VMEM((window, rows, cols), jnp.int32),
            pltpu.VMEM((window, fields + surface, LANES), BF16),
            pltpu.VMEM((members, fields + surface, LANES), BF16),
            pltpu.VMEM((total, fields, cols), F32),
            pltpu.VMEM((total, surface, cols), F32),
            pltpu.VMEM((total, surface, cols), F32),
            pltpu.VMEM((total, surface, cols), F32),
            pltpu.VMEM((fields + surface, LANES), F32),
            pltpu.VMEM((total, 3 * 2 * surface, cols), BF16),
            pltpu.VMEM((total, 3 * (fields + surface), cols), BF16),
            pltpu.VMEM((total, depth, cols), BF16),
            pltpu.VMEM((total, depth, cols), BF16),
            pltpu.VMEM((bands, flat, LANES), F32),
            pltpu.VMEM((bands, flat_sea, LANES), F32),
            pltpu.VMEM((bands, flat, LANES), BF16),
            pltpu.VMEM((members, flat, LANES), BF16),
            pltpu.VMEM((flat_sea, cols), BF16),
            pltpu.VMEM((members, flat_sea, cols), BF16),
            pltpu.VMEM((3 * hidden, tile_cols), F32),
            *[pltpu.VMEM(weight.shape, BF16) for weight in raw],
            pltpu.VMEM((hidden, round_up(9 * (fields + surface), LANES)), BF16),
            pltpu.VMEM((3 * hidden, air_depth), BF16),
            pltpu.VMEM((3 * (fields + surface), air_depth), BF16),
            pltpu.VMEM((hidden, round_up(9 * 2 * surface, LANES)), BF16),
            pltpu.VMEM((3 * surface, air_depth), BF16),
            dma((window, sections)),
            dma((window, bands)),
            dma((window, 3)),
            dma((window, 3)),
            dma((window, sections)),
            dma((window,)),
            dma((members,)),
            dma((members,)),
            dma((members,)),
            dma((members,)),
            dma((len(raw),)),
        ],
        compiler_params=pltpu.CompilerParams(
            collective_id=0, has_side_effects=True, vmem_limit_bytes=63 * 1024 * 1024
        ),
    )(
        atmosphere.reshape(members, flat, band_cols),
        ocean_state.reshape(members, flat_sea, cols),
        fluxes.reshape(members, flat_sea, cols),
        sea_mask,
        *raw,
    )
    return air.reshape(atmosphere.shape), sea.reshape(ocean_state.shape)


def solution(mesh):
    placed = (
        P(("grp", "mb"), None, "sp", "sec"),
        P(("grp", "mb"), None, "sp", None),
        P(("grp", "mb"), None, "sp", None),
        P("sp", None),
        P(),
        P(),
        P(),
        P(),
        P(),
    )
    return jax.shard_map(
        shards,
        mesh=mesh,
        in_specs=placed,
        out_specs=(P(("grp", "mb"), None, "sp", "sec"), P(("grp", "mb"), None, "sp", None)),
        check_vma=False,
    )
```

```python
import functools

import jax
import jax.numpy as jnp
from jax import lax
from jax.experimental import pallas as pl
from jax.experimental.pallas import tpu as pltpu
from jax.sharding import PartitionSpec as P

STEPS = 2
SEA_DILATIONS = (1, 1)
AIR_DILATIONS = (1, 2, 4)
LANES = 128
TILE_COLS = 1024
MESH = pl.DeviceIdType.MESH
F32 = jnp.float32
BF16 = jnp.bfloat16


def round_up(value, unit):
    return -(-value // unit) * unit


def rounded(value):
    return value.astype(BF16).astype(F32)


def gelu(v):
    half = 0.5 * v
    root = 0.7978845608028654
    return half + half * jnp.tanh(v * (root + (root * 0.044715) * (v * v)))


def kernel(
    dims,
    atm_ref, sea_ref, flux_ref, mask_ref, h_air1, h_air2, h_air3, h_sea1, h_sea2,
    air_out, sea_out,
    got_atm, got_sea, got_flux, got_mask, got_edge, edge_src,
    atm_f, sea_f, flux_f, mask_f, edge_f, wide_sea, wide_air, hidden_a, hidden_b,
    stage, stage_sea, fin_air_src, fin_air, fin_sea_src, fin_sea, product, spread,
    r_air1, r_air2, r_air3, r_sea1, r_sea2, w_air1, w_air2, w_air3, w_sea1, w_sea2,
    atm_send, atm_recv, near_send, near_recv, edge_send, edge_recv,
    fin_air_send, fin_air_recv, fin_sea_send, fin_sea_recv, weight_sem,
):
    sp, sections, members, rows, fields, surface, cols, window, home, hidden = dims
    bands = sections - 1
    total = window * rows
    own = home * rows
    me = lax.axis_index("sp")
    sec = lax.axis_index("sec")
    member = lax.rem(sec, members)
    base = sec - member
    in_band = sec < bands

    weight_copies = [
        pltpu.make_async_copy(src, dst, weight_sem.at[k])
        for k, (src, dst) in enumerate((
            (h_sea1, r_sea1), (h_sea2, r_sea2), (h_air1, r_air1), (h_air3, r_air3),
            (h_air2, r_air2),
        ))
    ]
    for copy in weight_copies:
        copy.start()

    def target_row(slot):
        return lax.rem(me - slot + home + 2 * sp, sp)

    lane = lax.broadcasted_iota(jnp.int32, (fields, LANES), 1)

    @pl.when(sec == bands)
    def _():
        for m in range(members):
            stage[0] = atm_ref[m].astype(F32)
            tile = jnp.zeros((fields, LANES), F32)
            for r in range(rows):
                line = stage[0, pl.ds(r, fields, stride=rows), :]
                line = line if r == 0 else pltpu.roll(line, r, 1)
                tile = jnp.where(lane == r, line, tile)
            edge_src[m] = jnp.concatenate(
                [tile, jnp.zeros((surface, LANES), F32)], axis=0
            ).astype(BF16)
        got_edge[home] = edge_src[member]

    @pl.when(in_band)
    def _():
        got_atm[home, jnp.minimum(sec, bands - 1)] = atm_ref[member]

    got_sea[home] = sea_ref[member]
    got_flux[home] = flux_ref[member]
    got_mask[home] = mask_ref[...]

    barrier = pltpu.get_barrier_semaphore()
    for slot in range(window):
        for to in range(sections):
            far = slot != home

            def greet(slot=slot, to=to):
                pl.semaphore_signal(
                    barrier, inc=1, device_id={"sp": target_row(slot), "sec": to},
                    device_id_type=MESH,
                )

            if far:
                greet()
            else:
                pl.when(sec != to)(greet)
    def lay_out(raw, laid, depth, outs):
        at = 0
        for low in range(0, depth, LANES):
            high = min(low + LANES, depth)
            panels = [[a] for a in range(3)] if high - low == LANES else [[0, 1, 2]]
            for taps in panels:
                columns = []
                for b in range(3):
                    parts = []
                    for a in taps:
                        parts.append(raw[3 * a + b, low:high, :].astype(F32))
                        spare = round_up(high - low, 16) - (high - low)
                        if spare:
                            parts.append(jnp.zeros((spare, outs), F32))
                    deep = sum(part.shape[0] for part in parts)
                    if deep < LANES:
                        parts.append(jnp.zeros((LANES - deep, outs), F32))
                    block = parts[0] if len(parts) == 1 else jnp.concatenate(parts, axis=0)
                    columns.append(block.T)
                laid[:, at:at + LANES] = jnp.concatenate(columns, axis=0).astype(BF16)
                at += LANES

    def pad_out(raw, laid):
        blank = jnp.zeros((raw.shape[0], laid.shape[1] - raw.shape[1]), BF16)
        laid[...] = jnp.concatenate([raw[...], blank], axis=1)

    def turn(raw, laid):
        depth = raw.shape[0]
        for low in range(0, depth, LANES):
            part = raw[low:min(low + LANES, depth), :].astype(F32)
            if part.shape[0] < LANES:
                spare = jnp.zeros((LANES - part.shape[0], part.shape[1]), F32)
                part = jnp.concatenate([part, spare], axis=0)
            laid[:, low:low + LANES] = part.T.astype(BF16)

    for copy in weight_copies:
        copy.wait()
    turn(r_sea1, w_sea1)
    lay_out(r_air2, w_air2, hidden, hidden)
    pl.semaphore_wait(barrier, window * sections - 1)

    def near_copies(slot):
        place = {"sp": target_row(slot), "sec": sec}
        pairs = (
            (sea_ref.at[member], got_sea.at[slot]),
            (flux_ref.at[member], got_flux.at[slot]),
            (mask_ref, got_mask.at[slot]),
        )
        return [
            pltpu.make_async_remote_copy(
                src_ref=src, dst_ref=dst,
                send_sem=near_send.at[slot, k], recv_sem=near_recv.at[slot, k],
                device_id=place, device_id_type=MESH,
            )
            for k, (src, dst) in enumerate(pairs)
        ]

    def atm_copy(slot, to, band):
        return pltpu.make_async_remote_copy(
            src_ref=atm_ref.at[to % members], dst_ref=got_atm.at[slot, band],
            send_sem=atm_send.at[slot, to], recv_sem=atm_recv.at[slot, band],
            device_id={"sp": target_row(slot), "sec": to}, device_id_type=MESH,
        )

    def edge_copy(slot, to):
        return pltpu.make_async_remote_copy(
            src_ref=edge_src.at[to % members], dst_ref=got_edge.at[slot],
            send_sem=edge_send.at[slot, to], recv_sem=edge_recv.at[slot],
            device_id={"sp": target_row(slot), "sec": to}, device_id_type=MESH,
        )

    slots = sorted(range(window), key=lambda slot: -abs(slot - home))
    for slot in slots:
        if slot != home:
            for copy in near_copies(slot):
                copy.start()

    def each_target(act):
        for slot in slots:
            for to in range(sections):
                if slot == home:
                    pl.when(sec != to)(functools.partial(act, slot, to))
                else:
                    act(slot, to)

    @pl.when(in_band)
    def _():
        band = jnp.minimum(sec, bands - 1)
        each_target(lambda slot, to: atm_copy(slot, to, band).start())

    @pl.when(sec == bands)
    def _():
        each_target(lambda slot, to: edge_copy(slot, to).start())

    column = lax.broadcasted_iota(jnp.int32, (1, cols), 1)
    tile_rows = max(1, TILE_COLS // cols)

    def span(margin):
        count = round_up(rows + 2 * margin, tile_rows)
        if count >= total:
            return 0, total
        return own - margin, count

    def conv(load, weight_ref, outs, dilation, margin, emit):
        start, count = span(margin)
        chunks = count // tile_rows

        def multiply(i):
            first = start + i * tile_rows + 2 * total
            pieces = []
            for t in range(tile_rows):
                taps = [load(lax.rem(first + t + (a - 1) * dilation, total)) for a in range(3)]
                pieces.append(jnp.concatenate([
                    part for level in zip(*taps) for part in level
                ], axis=0))
            block = pieces[0] if tile_rows == 1 else jnp.concatenate(pieces, axis=1)
            product[:weight_ref.shape[0]] = jnp.dot(
                weight_ref[:, :block.shape[0]], block, preferred_element_type=F32
            )

        def finish(i):
            first = start + i * tile_rows + 2 * total
            for t in range(tile_rows):
                part = slice(t * cols, (t + 1) * cols)
                if weight_ref.shape[0] == outs:
                    emit(lax.rem(first + t, total), product[:outs, part])
                    continue
                left = pltpu.roll(product[:outs, part], dilation, 1)
                right = pltpu.roll(product[2 * outs:3 * outs, part], cols - dilation, 1)
                value = product[outs:2 * outs, part]
                value = value + jnp.where(column >= dilation, left, 0.0)
                value = value + jnp.where(column < cols - dilation, right, 0.0)
                emit(lax.rem(first + t, total), value)

        def step(i, carry):
            finish(i)
            multiply(i + 1)
            return carry

        multiply(0)
        lax.fori_loop(0, chunks - 1, step, 0)
        finish(chunks - 1)

    last_lane = lax.broadcasted_iota(jnp.int32, (1, LANES), 1) == LANES - 1

    def widen(top, bottom, wide, rim=None):
        def step(i, carry):
            for t in range(rows):
                r = i * rows + t
                here = jnp.concatenate([top[r], bottom[r]], axis=0)
                left = jnp.where(column >= 1, pltpu.roll(here, 1, 1), 0.0)
                right = jnp.where(column < cols - 1, pltpu.roll(here, cols - 1, 1), 0.0)
                if rim is not None:
                    beside = jnp.where(last_lane, pltpu.roll(rim[...], LANES - 1 - r, 1), 0.0)
                    if cols > LANES:
                        blank = jnp.zeros((here.shape[0], cols - LANES), F32)
                        beside = jnp.concatenate([blank, beside], axis=1)
                    right = right + beside
                wide[r] = jnp.concatenate([left, here, right], axis=0).astype(BF16)
            return carry

        lax.fori_loop(0, window, step, 0)

    def conv_out(source, weight_ref, outs, dilation, margin, emit):
        begin, extent = span(margin + dilation)

        def multiply(i, carry):
            lines = [lax.rem(begin + i * tile_rows + t + 2 * total, total)
                     for t in range(tile_rows)]
            block = [source[r] for r in lines]
            block = block[0] if tile_rows == 1 else jnp.concatenate(block, axis=1)
            made = jnp.dot(
                weight_ref[:, :block.shape[0]], block, preferred_element_type=F32
            )
            for t in range(tile_rows):
                spread[lines[t], :9 * outs] = made[:, t * cols:(t + 1) * cols]
            return carry

        lax.fori_loop(0, extent // tile_rows, multiply, 0)
        start, count = span(margin)

        def finish(i, carry):
            for t in range(tile_rows):
                r = start + i * tile_rows + t + 2 * total
                lines = [lax.rem(r + (a - 1) * dilation, total) for a in range(3)]
                sums = []
                for b in range(3):
                    parts = [
                        spread[lines[a], (3 * a + b) * outs:(3 * a + b + 1) * outs]
                        for a in range(3)
                    ]
                    sums.append(parts[0] + parts[1] + parts[2])
                left = pltpu.roll(sums[0], dilation, 1)
                right = pltpu.roll(sums[2], cols - dilation, 1)
                value = sums[1] + jnp.where(column >= dilation, left, 0.0)
                value = value + jnp.where(column < cols - dilation, right, 0.0)
                emit(lines[1], value)
            return carry

        lax.fori_loop(0, count // tile_rows, finish, 0)

    def load_hidden(ref):
        return lambda r: [ref[r, at:min(at + LANES, ref.shape[1])]
                          for at in range(0, ref.shape[1], LANES)]

    def keep(ref):
        def emit(r, value):
            made = gelu(value)
            spare = jnp.zeros((ref.shape[1] - hidden, cols), F32)
            ref[r] = jnp.concatenate([made, spare], axis=0).astype(BF16)
        return emit

    def emit_sea(r, value):
        sea_f[r] = rounded(sea_f[r] + mask_f[r] * value)

    def emit_air3(r, value):
        atm_f[r] = rounded(atm_f[r] + value[:fields])
        flux_f[r] = rounded(value[fields:])

    pad_out(r_sea2, w_sea2)
    turn(r_air1, w_air1)
    pad_out(r_air3, w_air3)

    for slot in range(window):
        if slot != home:
            for copy in near_copies(slot):
                copy.wait_recv()
        for k, (got, state) in enumerate(((got_sea, sea_f), (got_flux, flux_f))):
            for band in range(bands):
                part = slice(band * LANES, (band + 1) * LANES)
                stage_sea[band] = got[slot, :, part].astype(F32)
                for r in range(rows):
                    state[slot * rows + r, :, part] = stage_sea[
                        band, pl.ds(r, surface, stride=rows), :
                    ]
        weight = got_mask[slot].astype(F32)
        for r in range(rows):
            mask_f[slot * rows + r] = jnp.broadcast_to(weight[r:r + 1], (surface, cols))

    def take_atmosphere():
        for slot in range(window):
            for band in range(bands):
                if slot == home:
                    pl.when(sec != band)(lambda: atm_copy(slot, 0, band).wait_recv())
                else:
                    atm_copy(slot, 0, band).wait_recv()
                stage[band] = got_atm[slot, band].astype(F32)
                for r in range(rows):
                    atm_f[slot * rows + r, :, band * LANES:(band + 1) * LANES] = stage[
                        band, pl.ds(r, fields, stride=rows), :
                    ]
            if slot == home:
                pl.when(sec != bands)(lambda: edge_copy(slot, 0).wait_recv())
            else:
                edge_copy(slot, 0).wait_recv()
        edge = jnp.zeros((fields + surface, LANES), F32)
        for slot in range(window):
            part = got_edge[slot].astype(F32)
            edge = edge + (part if slot == 0 else pltpu.roll(part, slot * rows, 1))
        edge_f[...] = edge

    halo = sum(SEA_DILATIONS) + sum(AIR_DILATIONS)
    for step in range(STEPS):
        after = (STEPS - 1 - step) * halo
        air = sum(AIR_DILATIONS)
        widen(sea_f, flux_f, wide_sea)
        conv(lambda r: [wide_sea[r]], w_sea1, hidden, 1, after + air + 1, keep(hidden_a))
        conv_out(hidden_a, w_sea2, surface, 1, after + air, emit_sea)
        if step == STEPS - 1:
            for band in range(bands):
                part = slice(band * LANES, (band + 1) * LANES)
                for r in range(rows):
                    stage_sea[band, pl.ds(r, surface, stride=rows), :] = sea_f[own + r, :, part]
                fin_sea_src[:, part] = stage_sea[band].astype(BF16)
            sea_copies = []
            for k in range(1, members):
                to = lax.rem(member + k, members)
                sea_copies.append(pltpu.make_async_remote_copy(
                    src_ref=fin_sea_src, dst_ref=fin_sea.at[member],
                    send_sem=fin_sea_send.at[k], recv_sem=fin_sea_recv.at[member],
                    device_id={"sec": base + to}, device_id_type=MESH,
                ))
                sea_copies[-1].start()
        if step == 0:
            take_atmosphere()
        widen(atm_f, sea_f, wide_air, edge_f)
        conv(lambda r: [wide_air[r]], w_air1, hidden, 1, after + 6, keep(hidden_a))
        conv(load_hidden(hidden_a), w_air2, hidden, 2, after + 4, keep(hidden_b))
        conv_out(hidden_b, w_air3, fields + surface, 4, after, emit_air3)

    for band in range(bands):
        for r in range(rows):
            stage[band, pl.ds(r, fields, stride=rows), :] = atm_f[
                own + r, :, band * LANES:(band + 1) * LANES
            ]
        fin_air_src[band] = stage[band].astype(BF16)

    def air_copy(k, landing):
        to = base + lax.rem(member + k, members)
        return to, pltpu.make_async_remote_copy(
            src_ref=fin_air_src.at[jnp.minimum(to, bands - 1)], dst_ref=fin_air.at[landing],
            send_sem=fin_air_send.at[k], recv_sem=fin_air_recv.at[landing],
            device_id={"sec": to}, device_id_type=MESH,
        )

    for k in range(1, members):
        to, copy = air_copy(k, member)
        pl.when(to < bands)(copy.start)

    sea_out[member] = fin_sea_src[...]
    for k in range(1, members):
        origin = lax.rem(member + k, members)
        pltpu.make_async_remote_copy(
            src_ref=fin_sea_src, dst_ref=fin_sea.at[origin],
            send_sem=fin_sea_send.at[k], recv_sem=fin_sea_recv.at[origin],
            device_id={"sec": base + origin}, device_id_type=MESH,
        ).wait_recv()
        sea_out[origin] = fin_sea[origin]

    @pl.when(sec == bands)
    def _():
        air_out[...] = atm_ref[...]

    @pl.when(in_band)
    def _():
        air_out[member] = fin_air_src[jnp.minimum(sec, bands - 1)]
        for k in range(1, members):
            origin = lax.rem(member + k, members)
            air_copy(k, origin)[1].wait_recv()
            air_out[origin] = fin_air[origin]

    for copy in sea_copies:
        copy.wait_send()
    for k in range(1, members):
        to, copy = air_copy(k, member)
        pl.when(to < bands)(copy.wait_send)
    for slot in slots:
        if slot != home:
            for copy in near_copies(slot):
                copy.wait_send()

    @pl.when(in_band)
    def _():
        band = jnp.minimum(sec, bands - 1)
        each_target(lambda slot, to: atm_copy(slot, to, band).wait_send())

    @pl.when(sec == bands)
    def _():
        each_target(lambda slot, to: edge_copy(slot, to).wait_send())


def taps_first(weight):
    return weight.reshape((-1,) + weight.shape[2:])


def shards(
    atmosphere, ocean_state, fluxes, sea_mask, air_entry, air_middle, air_exit, sea_entry, sea_exit
):
    sp = lax.axis_size("sp")
    sections = lax.axis_size("sec")
    bands = sections - 1
    members, fields, rows, band_cols = atmosphere.shape
    surface, cols = ocean_state.shape[1], ocean_state.shape[3]
    hidden = air_entry.shape[3]
    reach = STEPS * (sum(SEA_DILATIONS) + sum(AIR_DILATIONS))
    window = min(sp, 2 * (-(-reach // rows)) + 1)
    home = (window - 1) // 2
    total = window * rows
    depth = round_up(hidden, 16)
    assert band_cols == LANES and cols == bands * band_cols
    assert sections % members == 0 and total <= LANES and surface == fluxes.shape[1]
    dims = (sp, sections, members, rows, fields, surface, cols, window, home, hidden)
    dma = pltpu.SemaphoreType.DMA
    flat = fields * rows
    flat_sea = surface * rows
    raw = (
        air_entry.reshape(-1, hidden), taps_first(air_middle),
        taps_first(air_exit).transpose(0, 2, 1).reshape(-1, hidden),
        sea_entry.reshape(-1, hidden), taps_first(sea_exit).transpose(0, 2, 1).reshape(-1, hidden),
    )
    air_depth = LANES * (3 * (hidden // LANES) + 1)
    tile_cols = max(1, TILE_COLS // cols) * cols
    air, sea = pl.pallas_call(
        functools.partial(kernel, dims),
        out_shape=(
            jax.ShapeDtypeStruct((members, flat, band_cols), BF16),
            jax.ShapeDtypeStruct((members, flat_sea, cols), BF16),
        ),
        in_specs=[pl.BlockSpec(memory_space=pltpu.VMEM)] * 4
        + [pl.BlockSpec(memory_space=pl.ANY)] * 5,
        out_specs=(pl.BlockSpec(memory_space=pltpu.VMEM),) * 2,
        scratch_shapes=[
            pltpu.VMEM((window, bands, flat, LANES), BF16),
            pltpu.VMEM((window, flat_sea, cols), BF16),
            pltpu.VMEM((window, flat_sea, cols), BF16),
            pltpu.VMEM((window, rows, cols), jnp.int32),
            pltpu.VMEM((window, fields + surface, LANES), BF16),
            pltpu.VMEM((members, fields + surface, LANES), BF16),
            pltpu.VMEM((total, fields, cols), F32),
            pltpu.VMEM((total, surface, cols), F32),
            pltpu.VMEM((total, surface, cols), F32),
            pltpu.VMEM((total, surface, cols), F32),
            pltpu.VMEM((fields + surface, LANES), F32),
            pltpu.VMEM((total, 3 * 2 * surface, cols), BF16),
            pltpu.VMEM((total, 3 * (fields + surface), cols), BF16),
            pltpu.VMEM((total, depth, cols), BF16),
            pltpu.VMEM((total, depth, cols), BF16),
            pltpu.VMEM((bands, flat, LANES), F32),
            pltpu.VMEM((bands, flat_sea, LANES), F32),
            pltpu.VMEM((bands, flat, LANES), BF16),
            pltpu.VMEM((members, flat, LANES), BF16),
            pltpu.VMEM((flat_sea, cols), BF16),
            pltpu.VMEM((members, flat_sea, cols), BF16),
            pltpu.VMEM((3 * hidden, tile_cols), F32),
            pltpu.VMEM((total, 9 * (fields + surface), cols), F32),
            *[pltpu.VMEM(weight.shape, BF16) for weight in raw],
            pltpu.VMEM((hidden, round_up(9 * (fields + surface), LANES)), BF16),
            pltpu.VMEM((3 * hidden, air_depth), BF16),
            pltpu.VMEM((9 * (fields + surface), round_up(hidden, LANES)), BF16),
            pltpu.VMEM((hidden, round_up(9 * 2 * surface, LANES)), BF16),
            pltpu.VMEM((9 * surface, round_up(hidden, LANES)), BF16),
            dma((window, sections)),
            dma((window, bands)),
            dma((window, 3)),
            dma((window, 3)),
            dma((window, sections)),
            dma((window,)),
            dma((members,)),
            dma((members,)),
            dma((members,)),
            dma((members,)),
            dma((len(raw),)),
        ],
        compiler_params=pltpu.CompilerParams(
            collective_id=0, has_side_effects=True, vmem_limit_bytes=63 * 1024 * 1024
        ),
    )(
        atmosphere.reshape(members, flat, band_cols),
        ocean_state.reshape(members, flat_sea, cols),
        fluxes.reshape(members, flat_sea, cols),
        sea_mask,
        *raw,
    )
    return air.reshape(atmosphere.shape), sea.reshape(ocean_state.shape)


def solution(mesh):
    placed = (
        P(("grp", "mb"), None, "sp", "sec"),
        P(("grp", "mb"), None, "sp", None),
        P(("grp", "mb"), None, "sp", None),
        P("sp", None),
        P(),
        P(),
        P(),
        P(),
        P(),
    )
    return jax.shard_map(
        shards,
        mesh=mesh,
        in_specs=placed,
        out_specs=(P(("grp", "mb"), None, "sp", "sec"), P(("grp", "mb"), None, "sp", None)),
        check_vma=False,
    )
```

```python
import functools

import jax
import jax.numpy as jnp
from jax import lax
from jax.experimental import pallas as pl
from jax.experimental.pallas import tpu as pltpu
from jax.sharding import PartitionSpec as P

STEPS = 2
SEA_DILATIONS = (1, 1)
AIR_DILATIONS = (1, 2, 4)
LANES = 128
TILE_COLS = 1024
UNROLLED = 4
MESH = pl.DeviceIdType.MESH
F32 = jnp.float32
BF16 = jnp.bfloat16


def round_up(value, unit):
    return -(-value // unit) * unit


def wrapped(value, total):
    return value % total if isinstance(value, int) else lax.rem(value + 2 * total, total)


def each(count, body):
    if count <= UNROLLED:
        for i in range(count):
            body(i)
    else:
        lax.fori_loop(0, count, lambda i, carry: (body(i), carry)[1], 0)


def rounded(value):
    return value.astype(BF16).astype(F32)


def gelu(v):
    half = 0.5 * v
    root = 0.7978845608028654
    return half + half * jnp.tanh(v * (root + (root * 0.044715) * (v * v)))


def kernel(
    dims,
    atm_ref, sea_ref, flux_ref, mask_ref, h_air1, h_air2, h_air3, h_sea1, h_sea2,
    air_out, sea_out,
    got_atm, got_sea, got_flux, got_mask, got_edge, edge_src,
    atm_f, sea_f, flux_f, mask_f, edge_f, wide_sea, wide_air, hidden_a, hidden_b,
    stage, stage_sea, fin_air_src, fin_air, fin_sea_src, fin_sea, product,
    r_air1, r_air2, r_air3, r_sea1, r_sea2, w_air1, w_air2, w_air3, w_sea1, w_sea2,
    atm_send, atm_recv, near_send, near_recv, edge_send, edge_recv,
    fin_air_send, fin_air_recv, fin_sea_send, fin_sea_recv, weight_sem,
):
    sp, sections, members, rows, fields, surface, cols, window, home, hidden = dims
    bands = sections - 1
    total = window * rows
    own = home * rows
    me = lax.axis_index("sp")
    sec = lax.axis_index("sec")
    member = lax.rem(sec, members)
    base = sec - member
    in_band = sec < bands

    weight_copies = [
        pltpu.make_async_copy(src, dst, weight_sem.at[k])
        for k, (src, dst) in enumerate((
            (h_sea1, r_sea1), (h_sea2, r_sea2), (h_air1, r_air1), (h_air3, r_air3),
            (h_air2, r_air2),
        ))
    ]
    for copy in weight_copies:
        copy.start()

    def target_row(slot):
        return lax.rem(me - slot + home + 2 * sp, sp)

    lane = lax.broadcasted_iota(jnp.int32, (fields, LANES), 1)

    @pl.when(sec == bands)
    def _():
        for m in range(members):
            stage[0] = atm_ref[m].astype(F32)
            tile = jnp.zeros((fields, LANES), F32)
            for r in range(rows):
                line = stage[0, pl.ds(r, fields, stride=rows), :]
                line = line if r == 0 else pltpu.roll(line, r, 1)
                tile = jnp.where(lane == r, line, tile)
            edge_src[m] = jnp.concatenate(
                [tile, jnp.zeros((surface, LANES), F32)], axis=0
            ).astype(BF16)
        got_edge[home] = edge_src[member]

    @pl.when(in_band)
    def _():
        got_atm[home, jnp.minimum(sec, bands - 1)] = atm_ref[member]

    got_sea[home] = sea_ref[member]
    got_flux[home] = flux_ref[member]
    got_mask[home] = mask_ref[...]

    barrier = pltpu.get_barrier_semaphore()
    for slot in range(window):
        for to in range(sections):
            far = slot != home

            def greet(slot=slot, to=to):
                pl.semaphore_signal(
                    barrier, inc=1, device_id={"sp": target_row(slot), "sec": to},
                    device_id_type=MESH,
                )

            if far:
                greet()
            else:
                pl.when(sec != to)(greet)
    def lay_out(raw, laid, depth, outs, turned):
        at = 0
        for low in range(0, depth, LANES):
            high = min(low + LANES, depth)
            panels = [[a] for a in range(3)] if high - low == LANES else [[0, 1, 2]]
            for taps in panels:
                columns = []
                for b in range(3):
                    parts = []
                    for a in taps:
                        if turned:
                            part = raw[3 * a + b].astype(F32)[:, low:high]
                        else:
                            part = raw[3 * a + b, low:high, :].astype(F32)
                        spare = round_up(high - low, 16) - (high - low)
                        if spare:
                            shape = (outs, spare) if turned else (spare, outs)
                            part = jnp.concatenate(
                                [part, jnp.zeros(shape, F32)], axis=1 if turned else 0
                            )
                        parts.append(part)
                    axis = 1 if turned else 0
                    width = sum(part.shape[axis] for part in parts)
                    if width < LANES:
                        shape = (outs, LANES - width) if turned else (LANES - width, outs)
                        parts.append(jnp.zeros(shape, F32))
                    block = parts[0] if len(parts) == 1 else jnp.concatenate(parts, axis=axis)
                    columns.append(block if turned else block.T)
                laid[:, at:at + LANES] = jnp.concatenate(columns, axis=0).astype(BF16)
                at += LANES

    def turn(raw, laid):
        depth = raw.shape[0]
        for low in range(0, depth, LANES):
            part = raw[low:min(low + LANES, depth), :].astype(F32)
            if part.shape[0] < LANES:
                spare = jnp.zeros((LANES - part.shape[0], part.shape[1]), F32)
                part = jnp.concatenate([part, spare], axis=0)
            laid[:, low:low + LANES] = part.T.astype(BF16)

    for copy in weight_copies:
        copy.wait()
    turn(r_sea1, w_sea1)
    lay_out(r_air2, w_air2, hidden, hidden, False)
    pl.semaphore_wait(barrier, window * sections - 1)

    def near_copies(slot):
        place = {"sp": target_row(slot), "sec": sec}
        pairs = (
            (sea_ref.at[member], got_sea.at[slot]),
            (flux_ref.at[member], got_flux.at[slot]),
            (mask_ref, got_mask.at[slot]),
        )
        return [
            pltpu.make_async_remote_copy(
                src_ref=src, dst_ref=dst,
                send_sem=near_send.at[slot, k], recv_sem=near_recv.at[slot, k],
                device_id=place, device_id_type=MESH,
            )
            for k, (src, dst) in enumerate(pairs)
        ]

    def atm_copy(slot, to, band):
        return pltpu.make_async_remote_copy(
            src_ref=atm_ref.at[to % members], dst_ref=got_atm.at[slot, band],
            send_sem=atm_send.at[slot, to], recv_sem=atm_recv.at[slot, band],
            device_id={"sp": target_row(slot), "sec": to}, device_id_type=MESH,
        )

    def edge_copy(slot, to):
        return pltpu.make_async_remote_copy(
            src_ref=edge_src.at[to % members], dst_ref=got_edge.at[slot],
            send_sem=edge_send.at[slot, to], recv_sem=edge_recv.at[slot],
            device_id={"sp": target_row(slot), "sec": to}, device_id_type=MESH,
        )

    slots = sorted(range(window), key=lambda slot: -abs(slot - home))
    for slot in slots:
        if slot != home:
            for copy in near_copies(slot):
                copy.start()

    def each_target(act):
        for slot in slots:
            for to in range(sections):
                if slot == home:
                    pl.when(sec != to)(functools.partial(act, slot, to))
                else:
                    act(slot, to)

    @pl.when(in_band)
    def _():
        band = jnp.minimum(sec, bands - 1)
        each_target(lambda slot, to: atm_copy(slot, to, band).start())

    @pl.when(sec == bands)
    def _():
        each_target(lambda slot, to: edge_copy(slot, to).start())

    column = lax.broadcasted_iota(jnp.int32, (1, cols), 1)
    tile_rows = max(1, TILE_COLS // cols)

    def span(margin):
        count = round_up(rows + 2 * margin, tile_rows)
        if count >= total:
            return 0, total
        return own - margin, count

    def conv(load, weight_ref, outs, dilation, margin, emit):
        start, count = span(margin)
        chunks = count // tile_rows

        def multiply(i, made):
            first = start + i * tile_rows
            pieces = []
            for t in range(tile_rows):
                taps = [load(wrapped(first + t + (a - 1) * dilation, total)) for a in range(3)]
                pieces.append(jnp.concatenate([
                    part for level in zip(*taps) for part in level
                ], axis=0))
            block = pieces[0] if tile_rows == 1 else jnp.concatenate(pieces, axis=1)
            made[:weight_ref.shape[0]] = jnp.dot(
                weight_ref[:, :block.shape[0]], block, preferred_element_type=F32
            )

        def finish(i, made):
            first = start + i * tile_rows
            for t in range(tile_rows):
                part = slice(t * cols, (t + 1) * cols)
                if weight_ref.shape[0] == outs:
                    emit(wrapped(first + t, total), made[:outs, part])
                    continue
                left = pltpu.roll(made[:outs, part], dilation, 1)
                right = pltpu.roll(made[2 * outs:3 * outs, part], cols - dilation, 1)
                value = made[outs:2 * outs, part]
                value = value + jnp.where(column >= dilation, left, 0.0)
                value = value + jnp.where(column < cols - dilation, right, 0.0)
                emit(wrapped(first + t, total), value)

        if chunks <= UNROLLED:
            multiply(0, product.at[0])
            for i in range(chunks):
                if i + 1 < chunks:
                    multiply(i + 1, product.at[(i + 1) % 2])
                finish(i, product.at[i % 2])
            return

        def step(i):
            finish(i, product.at[0])
            multiply(i + 1, product.at[0])

        multiply(0, product.at[0])
        each(chunks - 1, step)
        finish(chunks - 1, product.at[0])

    last_lane = lax.broadcasted_iota(jnp.int32, (1, LANES), 1) == LANES - 1

    def widen(top, bottom, wide, rim=None):
        def step(i):
            for t in range(rows):
                r = i * rows + t
                here = jnp.concatenate([top[r], bottom[r]], axis=0)
                left = jnp.where(column >= 1, pltpu.roll(here, 1, 1), 0.0)
                right = jnp.where(column < cols - 1, pltpu.roll(here, cols - 1, 1), 0.0)
                if rim is not None:
                    beside = jnp.where(last_lane, pltpu.roll(rim[...], LANES - 1 - r, 1), 0.0)
                    if cols > LANES:
                        blank = jnp.zeros((here.shape[0], cols - LANES), F32)
                        beside = jnp.concatenate([blank, beside], axis=1)
                    right = right + beside
                wide[r] = jnp.concatenate([left, here, right], axis=0).astype(BF16)

        each(window, step)

    def load_hidden(ref):
        return lambda r: [ref[r, at:min(at + LANES, ref.shape[1])]
                          for at in range(0, ref.shape[1], LANES)]

    def keep(ref):
        def emit(r, value):
            made = gelu(value)
            spare = jnp.zeros((ref.shape[1] - hidden, cols), F32)
            ref[r] = jnp.concatenate([made, spare], axis=0).astype(BF16)
        return emit

    def emit_sea(r, value):
        sea_f[r] = rounded(sea_f[r] + mask_f[r] * value)

    def emit_air3(r, value):
        atm_f[r] = rounded(atm_f[r] + value[:fields])
        flux_f[r] = rounded(value[fields:])

    lay_out(r_sea2, w_sea2, hidden, surface, True)
    turn(r_air1, w_air1)
    lay_out(r_air3, w_air3, hidden, fields + surface, True)

    for slot in range(window):
        if slot != home:
            for copy in near_copies(slot):
                copy.wait_recv()
        for k, (got, state) in enumerate(((got_sea, sea_f), (got_flux, flux_f))):
            for band in range(bands):
                part = slice(band * LANES, (band + 1) * LANES)
                stage_sea[band] = got[slot, :, part].astype(F32)
                for r in range(rows):
                    state[slot * rows + r, :, part] = stage_sea[
                        band, pl.ds(r, surface, stride=rows), :
                    ]
        weight = got_mask[slot].astype(F32)
        for r in range(rows):
            mask_f[slot * rows + r] = jnp.broadcast_to(weight[r:r + 1], (surface, cols))

    def take_atmosphere():
        for slot in range(window):
            for band in range(bands):
                if slot == home:
                    pl.when(sec != band)(lambda: atm_copy(slot, 0, band).wait_recv())
                else:
                    atm_copy(slot, 0, band).wait_recv()
                stage[band] = got_atm[slot, band].astype(F32)
                for r in range(rows):
                    atm_f[slot * rows + r, :, band * LANES:(band + 1) * LANES] = stage[
                        band, pl.ds(r, fields, stride=rows), :
                    ]
            if slot == home:
                pl.when(sec != bands)(lambda: edge_copy(slot, 0).wait_recv())
            else:
                edge_copy(slot, 0).wait_recv()
        edge = jnp.zeros((fields + surface, LANES), F32)
        for slot in range(window):
            part = got_edge[slot].astype(F32)
            edge = edge + (part if slot == 0 else pltpu.roll(part, slot * rows, 1))
        edge_f[...] = edge

    halo = sum(SEA_DILATIONS) + sum(AIR_DILATIONS)
    for step in range(STEPS):
        after = (STEPS - 1 - step) * halo
        air = sum(AIR_DILATIONS)
        widen(sea_f, flux_f, wide_sea)
        conv(lambda r: [wide_sea[r]], w_sea1, hidden, 1, after + air + 1, keep(hidden_a))
        conv(load_hidden(hidden_a), w_sea2, surface, 1, after + air, emit_sea)
        if step == STEPS - 1:
            for band in range(bands):
                part = slice(band * LANES, (band + 1) * LANES)
                for r in range(rows):
                    stage_sea[band, pl.ds(r, surface, stride=rows), :] = sea_f[own + r, :, part]
                fin_sea_src[:, part] = stage_sea[band].astype(BF16)
            sea_copies = []
            for k in range(1, members):
                to = lax.rem(member + k, members)
                sea_copies.append(pltpu.make_async_remote_copy(
                    src_ref=fin_sea_src, dst_ref=fin_sea.at[member],
                    send_sem=fin_sea_send.at[k], recv_sem=fin_sea_recv.at[member],
                    device_id={"sec": base + to}, device_id_type=MESH,
                ))
                sea_copies[-1].start()
        if step == 0:
            take_atmosphere()
        widen(atm_f, sea_f, wide_air, edge_f)
        conv(lambda r: [wide_air[r]], w_air1, hidden, 1, after + 6, keep(hidden_a))
        conv(load_hidden(hidden_a), w_air2, hidden, 2, after + 4, keep(hidden_b))
        conv(load_hidden(hidden_b), w_air3, fields + surface, 4, after, emit_air3)

    for band in range(bands):
        for r in range(rows):
            stage[band, pl.ds(r, fields, stride=rows), :] = atm_f[
                own + r, :, band * LANES:(band + 1) * LANES
            ]
        fin_air_src[band] = stage[band].astype(BF16)

    def air_copy(k, landing):
        to = base + lax.rem(member + k, members)
        return to, pltpu.make_async_remote_copy(
            src_ref=fin_air_src.at[jnp.minimum(to, bands - 1)], dst_ref=fin_air.at[landing],
            send_sem=fin_air_send.at[k], recv_sem=fin_air_recv.at[landing],
            device_id={"sec": to}, device_id_type=MESH,
        )

    for k in range(1, members):
        to, copy = air_copy(k, member)
        pl.when(to < bands)(copy.start)

    sea_out[member] = fin_sea_src[...]
    for k in range(1, members):
        origin = lax.rem(member + k, members)
        pltpu.make_async_remote_copy(
            src_ref=fin_sea_src, dst_ref=fin_sea.at[origin],
            send_sem=fin_sea_send.at[k], recv_sem=fin_sea_recv.at[origin],
            device_id={"sec": base + origin}, device_id_type=MESH,
        ).wait_recv()
        sea_out[origin] = fin_sea[origin]

    @pl.when(sec == bands)
    def _():
        air_out[...] = atm_ref[...]

    @pl.when(in_band)
    def _():
        air_out[member] = fin_air_src[jnp.minimum(sec, bands - 1)]
        for k in range(1, members):
            origin = lax.rem(member + k, members)
            air_copy(k, origin)[1].wait_recv()
            air_out[origin] = fin_air[origin]

    for copy in sea_copies:
        copy.wait_send()
    for k in range(1, members):
        to, copy = air_copy(k, member)
        pl.when(to < bands)(copy.wait_send)
    for slot in slots:
        if slot != home:
            for copy in near_copies(slot):
                copy.wait_send()

    @pl.when(in_band)
    def _():
        band = jnp.minimum(sec, bands - 1)
        each_target(lambda slot, to: atm_copy(slot, to, band).wait_send())

    @pl.when(sec == bands)
    def _():
        each_target(lambda slot, to: edge_copy(slot, to).wait_send())


def taps_first(weight):
    return weight.reshape((-1,) + weight.shape[2:])


def shards(
    atmosphere, ocean_state, fluxes, sea_mask, air_entry, air_middle, air_exit, sea_entry, sea_exit
):
    sp = lax.axis_size("sp")
    sections = lax.axis_size("sec")
    bands = sections - 1
    members, fields, rows, band_cols = atmosphere.shape
    surface, cols = ocean_state.shape[1], ocean_state.shape[3]
    hidden = air_entry.shape[3]
    reach = STEPS * (sum(SEA_DILATIONS) + sum(AIR_DILATIONS))
    window = min(sp, 2 * (-(-reach // rows)) + 1)
    home = (window - 1) // 2
    total = window * rows
    depth = round_up(hidden, 16)
    assert band_cols == LANES and cols == bands * band_cols
    assert sections % members == 0 and total <= LANES and surface == fluxes.shape[1]
    dims = (sp, sections, members, rows, fields, surface, cols, window, home, hidden)
    dma = pltpu.SemaphoreType.DMA
    flat = fields * rows
    flat_sea = surface * rows
    raw = (
        air_entry.reshape(-1, hidden), taps_first(air_middle),
        taps_first(air_exit).transpose(0, 2, 1),
        sea_entry.reshape(-1, hidden), taps_first(sea_exit).transpose(0, 2, 1),
    )
    air_depth = LANES * (3 * (hidden // LANES) + 1)
    tile_cols = max(1, TILE_COLS // cols) * cols
    air, sea = pl.pallas_call(
        functools.partial(kernel, dims),
        out_shape=(
            jax.ShapeDtypeStruct((members, flat, band_cols), BF16),
            jax.ShapeDtypeStruct((members, flat_sea, cols), BF16),
        ),
        in_specs=[pl.BlockSpec(memory_space=pltpu.VMEM)] * 4
        + [pl.BlockSpec(memory_space=pl.ANY)] * 5,
        out_specs=(pl.BlockSpec(memory_space=pltpu.VMEM),) * 2,
        scratch_shapes=[
            pltpu.VMEM((window, bands, flat, LANES), BF16),
            pltpu.VMEM((window, flat_sea, cols), BF16),
            pltpu.VMEM((window, flat_sea, cols), BF16),
            pltpu.VMEM((window, rows, cols), jnp.int32),
            pltpu.VMEM((window, fields + surface, LANES), BF16),
            pltpu.VMEM((members, fields + surface, LANES), BF16),
            pltpu.VMEM((total, fields, cols), F32),
            pltpu.VMEM((total, surface, cols), F32),
            pltpu.VMEM((total, surface, cols), F32),
            pltpu.VMEM((total, surface, cols), F32),
            pltpu.VMEM((fields + surface, LANES), F32),
            pltpu.VMEM((total, 3 * 2 * surface, cols), BF16),
            pltpu.VMEM((total, 3 * (fields + surface), cols), BF16),
            pltpu.VMEM((total, depth, cols), BF16),
            pltpu.VMEM((total, depth, cols), BF16),
            pltpu.VMEM((bands, flat, LANES), F32),
            pltpu.VMEM((bands, flat_sea, LANES), F32),
            pltpu.VMEM((bands, flat, LANES), BF16),
            pltpu.VMEM((members, flat, LANES), BF16),
            pltpu.VMEM((flat_sea, cols), BF16),
            pltpu.VMEM((members, flat_sea, cols), BF16),
            pltpu.VMEM((2, 3 * hidden, tile_cols), F32),
            *[pltpu.VMEM(weight.shape, BF16) for weight in raw],
            pltpu.VMEM((hidden, round_up(9 * (fields + surface), LANES)), BF16),
            pltpu.VMEM((3 * hidden, air_depth), BF16),
            pltpu.VMEM((3 * (fields + surface), air_depth), BF16),
            pltpu.VMEM((hidden, round_up(9 * 2 * surface, LANES)), BF16),
            pltpu.VMEM((3 * surface, air_depth), BF16),
            dma((window, sections)),
            dma((window, bands)),
            dma((window, 3)),
            dma((window, 3)),
            dma((window, sections)),
            dma((window,)),
            dma((members,)),
            dma((members,)),
            dma((members,)),
            dma((members,)),
            dma((len(raw),)),
        ],
        compiler_params=pltpu.CompilerParams(
            collective_id=0, has_side_effects=True, vmem_limit_bytes=63 * 1024 * 1024
        ),
    )(
        atmosphere.reshape(members, flat, band_cols),
        ocean_state.reshape(members, flat_sea, cols),
        fluxes.reshape(members, flat_sea, cols),
        sea_mask,
        *raw,
    )
    return air.reshape(atmosphere.shape), sea.reshape(ocean_state.shape)


def solution(mesh):
    placed = (
        P(("grp", "mb"), None, "sp", "sec"),
        P(("grp", "mb"), None, "sp", None),
        P(("grp", "mb"), None, "sp", None),
        P("sp", None),
        P(),
        P(),
        P(),
        P(),
        P(),
    )
    return jax.shard_map(
        shards,
        mesh=mesh,
        in_specs=placed,
        out_specs=(P(("grp", "mb"), None, "sp", "sec"), P(("grp", "mb"), None, "sp", None)),
        check_vma=False,
    )
```

```python
import functools

import jax
import jax.numpy as jnp
from jax import lax
from jax.experimental import pallas as pl
from jax.experimental.pallas import tpu as pltpu
from jax.sharding import PartitionSpec as P

STEPS = 2
SEA_DILATIONS = (1, 1)
AIR_DILATIONS = (1, 2, 4)
LANES = 128
TILE_COLS = 512
UNROLLED = 8
MESH = pl.DeviceIdType.MESH
F32 = jnp.float32
BF16 = jnp.bfloat16


def round_up(value, unit):
    return -(-value // unit) * unit


def wrapped(value, total):
    return value % total if isinstance(value, int) else lax.rem(value + 2 * total, total)


def each(count, body):
    if count <= UNROLLED:
        for i in range(count):
            body(i)
    else:
        lax.fori_loop(0, count, lambda i, carry: (body(i), carry)[1], 0)


def rounded(value):
    return value.astype(BF16).astype(F32)


def gelu(v):
    half = 0.5 * v
    root = 0.7978845608028654
    return half + half * jnp.tanh(v * (root + (root * 0.044715) * (v * v)))


def kernel(
    dims,
    atm_ref, sea_ref, flux_ref, mask_ref, h_air1, h_air2, h_air3, h_sea1, h_sea2,
    air_out, sea_out,
    got_atm, got_sea, got_flux, got_mask, got_edge, edge_src,
    atm_f, sea_f, flux_f, mask_f, edge_f, wide_sea, wide_air, hidden_a, hidden_b,
    stage, stage_sea, fin_air_src, fin_air, fin_sea_src, fin_sea, product,
    r_air1, r_air2, r_air3, r_sea1, r_sea2, w_air1, w_air2, w_air3, w_sea1, w_sea2,
    atm_send, atm_recv, near_send, near_recv, edge_send, edge_recv,
    fin_air_send, fin_air_recv, fin_sea_send, fin_sea_recv, weight_sem,
):
    sp, sections, members, rows, fields, surface, cols, window, home, hidden = dims
    bands = sections - 1
    total = window * rows
    own = home * rows
    me = lax.axis_index("sp")
    sec = lax.axis_index("sec")
    member = lax.rem(sec, members)
    base = sec - member
    in_band = sec < bands

    weight_copies = [
        pltpu.make_async_copy(src, dst, weight_sem.at[k])
        for k, (src, dst) in enumerate((
            (h_sea1, r_sea1), (h_sea2, r_sea2), (h_air1, r_air1), (h_air3, r_air3),
            (h_air2, r_air2),
        ))
    ]
    for copy in weight_copies:
        copy.start()

    def target_row(slot):
        return lax.rem(me - slot + home + 2 * sp, sp)

    lane = lax.broadcasted_iota(jnp.int32, (fields, LANES), 1)

    @pl.when(sec == bands)
    def _():
        for m in range(members):
            stage[0] = atm_ref[m].astype(F32)
            tile = jnp.zeros((fields, LANES), F32)
            for r in range(rows):
                line = stage[0, pl.ds(r, fields, stride=rows), :]
                line = line if r == 0 else pltpu.roll(line, r, 1)
                tile = jnp.where(lane == r, line, tile)
            edge_src[m] = jnp.concatenate(
                [tile, jnp.zeros((surface, LANES), F32)], axis=0
            ).astype(BF16)
        got_edge[home] = edge_src[member]

    @pl.when(in_band)
    def _():
        got_atm[home, jnp.minimum(sec, bands - 1)] = atm_ref[member]

    got_sea[home] = sea_ref[member]
    got_flux[home] = flux_ref[member]
    got_mask[home] = mask_ref[...]

    barrier = pltpu.get_barrier_semaphore()
    for slot in range(window):
        for to in range(sections):
            far = slot != home

            def greet(slot=slot, to=to):
                pl.semaphore_signal(
                    barrier, inc=1, device_id={"sp": target_row(slot), "sec": to},
                    device_id_type=MESH,
                )

            if far:
                greet()
            else:
                pl.when(sec != to)(greet)
    def lay_out(raw, laid, depth, outs, turned):
        at = 0
        for low in range(0, depth, LANES):
            high = min(low + LANES, depth)
            panels = [[a] for a in range(3)] if high - low == LANES else [[0, 1, 2]]
            for taps in panels:
                columns = []
                for b in range(3):
                    parts = []
                    for a in taps:
                        if turned:
                            part = raw[3 * a + b].astype(F32)[:, low:high]
                        else:
                            part = raw[3 * a + b, low:high, :].astype(F32)
                        spare = round_up(high - low, 16) - (high - low)
                        if spare:
                            shape = (outs, spare) if turned else (spare, outs)
                            part = jnp.concatenate(
                                [part, jnp.zeros(shape, F32)], axis=1 if turned else 0
                            )
                        parts.append(part)
                    axis = 1 if turned else 0
                    width = sum(part.shape[axis] for part in parts)
                    if width < LANES:
                        shape = (outs, LANES - width) if turned else (LANES - width, outs)
                        parts.append(jnp.zeros(shape, F32))
                    block = parts[0] if len(parts) == 1 else jnp.concatenate(parts, axis=axis)
                    columns.append(block if turned else block.T)
                laid[:, at:at + LANES] = jnp.concatenate(columns, axis=0).astype(BF16)
                at += LANES

    def turn(raw, laid):
        depth = raw.shape[0]
        for low in range(0, depth, LANES):
            part = raw[low:min(low + LANES, depth), :].astype(F32)
            if part.shape[0] < LANES:
                spare = jnp.zeros((LANES - part.shape[0], part.shape[1]), F32)
                part = jnp.concatenate([part, spare], axis=0)
            laid[:, low:low + LANES] = part.T.astype(BF16)

    for copy in weight_copies:
        copy.wait()
    turn(r_sea1, w_sea1)
    lay_out(r_air2, w_air2, hidden, hidden, False)
    pl.semaphore_wait(barrier, window * sections - 1)

    def near_copies(slot):
        place = {"sp": target_row(slot), "sec": sec}
        pairs = (
            (sea_ref.at[member], got_sea.at[slot]),
            (flux_ref.at[member], got_flux.at[slot]),
            (mask_ref, got_mask.at[slot]),
        )
        return [
            pltpu.make_async_remote_copy(
                src_ref=src, dst_ref=dst,
                send_sem=near_send.at[slot, k], recv_sem=near_recv.at[slot, k],
                device_id=place, device_id_type=MESH,
            )
            for k, (src, dst) in enumerate(pairs)
        ]

    def atm_copy(slot, to, band):
        return pltpu.make_async_remote_copy(
            src_ref=atm_ref.at[to % members], dst_ref=got_atm.at[slot, band],
            send_sem=atm_send.at[slot, to], recv_sem=atm_recv.at[slot, band],
            device_id={"sp": target_row(slot), "sec": to}, device_id_type=MESH,
        )

    def edge_copy(slot, to):
        return pltpu.make_async_remote_copy(
            src_ref=edge_src.at[to % members], dst_ref=got_edge.at[slot],
            send_sem=edge_send.at[slot, to], recv_sem=edge_recv.at[slot],
            device_id={"sp": target_row(slot), "sec": to}, device_id_type=MESH,
        )

    slots = sorted(range(window), key=lambda slot: -abs(slot - home))
    for slot in slots:
        if slot != home:
            for copy in near_copies(slot):
                copy.start()

    def each_target(act):
        for slot in slots:
            for to in range(sections):
                if slot == home:
                    pl.when(sec != to)(functools.partial(act, slot, to))
                else:
                    act(slot, to)

    @pl.when(in_band)
    def _():
        band = jnp.minimum(sec, bands - 1)
        each_target(lambda slot, to: atm_copy(slot, to, band).start())

    @pl.when(sec == bands)
    def _():
        each_target(lambda slot, to: edge_copy(slot, to).start())

    column = lax.broadcasted_iota(jnp.int32, (1, cols), 1)
    tile_rows = max(1, TILE_COLS // cols)

    def span(margin):
        count = round_up(rows + 2 * margin, tile_rows)
        if count >= total:
            return 0, total
        return own - margin, count

    def conv(load, weight_ref, outs, dilation, margin, emit):
        start, count = span(margin)
        chunks = count // tile_rows

        def multiply(i, made):
            first = start + i * tile_rows
            pieces = []
            for t in range(tile_rows):
                taps = [load(wrapped(first + t + (a - 1) * dilation, total)) for a in range(3)]
                pieces.append(jnp.concatenate([
                    part for level in zip(*taps) for part in level
                ], axis=0))
            block = pieces[0] if tile_rows == 1 else jnp.concatenate(pieces, axis=1)
            made[:weight_ref.shape[0]] = jnp.dot(
                weight_ref[:, :block.shape[0]], block, preferred_element_type=F32
            )

        def finish(i, made):
            first = start + i * tile_rows
            for t in range(tile_rows):
                part = slice(t * cols, (t + 1) * cols)
                if weight_ref.shape[0] == outs:
                    emit(wrapped(first + t, total), made[:outs, part])
                    continue
                left = pltpu.roll(made[:outs, part], dilation, 1)
                right = pltpu.roll(made[2 * outs:3 * outs, part], cols - dilation, 1)
                value = made[outs:2 * outs, part]
                value = value + jnp.where(column >= dilation, left, 0.0)
                value = value + jnp.where(column < cols - dilation, right, 0.0)
                emit(wrapped(first + t, total), value)

        if chunks <= UNROLLED:
            multiply(0, product.at[0])
            for i in range(chunks):
                if i + 1 < chunks:
                    multiply(i + 1, product.at[(i + 1) % 2])
                finish(i, product.at[i % 2])
            return

        def step(i):
            finish(i, product.at[0])
            multiply(i + 1, product.at[0])

        multiply(0, product.at[0])
        each(chunks - 1, step)
        finish(chunks - 1, product.at[0])

    last_lane = lax.broadcasted_iota(jnp.int32, (1, LANES), 1) == LANES - 1

    def widen(top, bottom, wide, rim=None):
        def step(i):
            for t in range(rows):
                r = i * rows + t
                here = jnp.concatenate([top[r], bottom[r]], axis=0)
                left = jnp.where(column >= 1, pltpu.roll(here, 1, 1), 0.0)
                right = jnp.where(column < cols - 1, pltpu.roll(here, cols - 1, 1), 0.0)
                if rim is not None:
                    beside = jnp.where(last_lane, pltpu.roll(rim[...], LANES - 1 - r, 1), 0.0)
                    if cols > LANES:
                        blank = jnp.zeros((here.shape[0], cols - LANES), F32)
                        beside = jnp.concatenate([blank, beside], axis=1)
                    right = right + beside
                wide[r] = jnp.concatenate([left, here, right], axis=0).astype(BF16)

        each(window, step)

    def load_hidden(ref):
        return lambda r: [ref[r, at:min(at + LANES, ref.shape[1])]
                          for at in range(0, ref.shape[1], LANES)]

    def keep(ref):
        def emit(r, value):
            made = gelu(value)
            spare = jnp.zeros((ref.shape[1] - hidden, cols), F32)
            ref[r] = jnp.concatenate([made, spare], axis=0).astype(BF16)
        return emit

    def emit_sea(r, value):
        sea_f[r] = rounded(sea_f[r] + mask_f[r] * value)

    def emit_air3(r, value):
        atm_f[r] = rounded(atm_f[r] + value[:fields])
        flux_f[r] = rounded(value[fields:])

    lay_out(r_sea2, w_sea2, hidden, surface, True)
    turn(r_air1, w_air1)
    lay_out(r_air3, w_air3, hidden, fields + surface, True)

    for slot in range(window):
        if slot != home:
            for copy in near_copies(slot):
                copy.wait_recv()
        for k, (got, state) in enumerate(((got_sea, sea_f), (got_flux, flux_f))):
            for band in range(bands):
                part = slice(band * LANES, (band + 1) * LANES)
                stage_sea[band] = got[slot, :, part].astype(F32)
                for r in range(rows):
                    state[slot * rows + r, :, part] = stage_sea[
                        band, pl.ds(r, surface, stride=rows), :
                    ]
        weight = got_mask[slot].astype(F32)
        for r in range(rows):
            mask_f[slot * rows + r] = jnp.broadcast_to(weight[r:r + 1], (surface, cols))

    def take_atmosphere():
        for slot in range(window):
            for band in range(bands):
                if slot == home:
                    pl.when(sec != band)(lambda: atm_copy(slot, 0, band).wait_recv())
                else:
                    atm_copy(slot, 0, band).wait_recv()
                stage[band] = got_atm[slot, band].astype(F32)
                for r in range(rows):
                    atm_f[slot * rows + r, :, band * LANES:(band + 1) * LANES] = stage[
                        band, pl.ds(r, fields, stride=rows), :
                    ]
            if slot == home:
                pl.when(sec != bands)(lambda: edge_copy(slot, 0).wait_recv())
            else:
                edge_copy(slot, 0).wait_recv()
        edge = jnp.zeros((fields + surface, LANES), F32)
        for slot in range(window):
            part = got_edge[slot].astype(F32)
            edge = edge + (part if slot == 0 else pltpu.roll(part, slot * rows, 1))
        edge_f[...] = edge

    halo = sum(SEA_DILATIONS) + sum(AIR_DILATIONS)
    for step in range(STEPS):
        after = (STEPS - 1 - step) * halo
        air = sum(AIR_DILATIONS)
        widen(sea_f, flux_f, wide_sea)
        conv(lambda r: [wide_sea[r]], w_sea1, hidden, 1, after + air + 1, keep(hidden_a))
        conv(load_hidden(hidden_a), w_sea2, surface, 1, after + air, emit_sea)
        if step == STEPS - 1:
            for band in range(bands):
                part = slice(band * LANES, (band + 1) * LANES)
                for r in range(rows):
                    stage_sea[band, pl.ds(r, surface, stride=rows), :] = sea_f[own + r, :, part]
                fin_sea_src[:, part] = stage_sea[band].astype(BF16)
            sea_copies = []
            for k in range(1, members):
                to = lax.rem(member + k, members)
                sea_copies.append(pltpu.make_async_remote_copy(
                    src_ref=fin_sea_src, dst_ref=fin_sea.at[member],
                    send_sem=fin_sea_send.at[k], recv_sem=fin_sea_recv.at[member],
                    device_id={"sec": base + to}, device_id_type=MESH,
                ))
                sea_copies[-1].start()
        if step == 0:
            take_atmosphere()
        widen(atm_f, sea_f, wide_air, edge_f)
        conv(lambda r: [wide_air[r]], w_air1, hidden, 1, after + 6, keep(hidden_a))
        conv(load_hidden(hidden_a), w_air2, hidden, 2, after + 4, keep(hidden_b))
        conv(load_hidden(hidden_b), w_air3, fields + surface, 4, after, emit_air3)

    for band in range(bands):
        for r in range(rows):
            stage[band, pl.ds(r, fields, stride=rows), :] = atm_f[
                own + r, :, band * LANES:(band + 1) * LANES
            ]
        fin_air_src[band] = stage[band].astype(BF16)

    def air_copy(k, landing):
        to = base + lax.rem(member + k, members)
        return to, pltpu.make_async_remote_copy(
            src_ref=fin_air_src.at[jnp.minimum(to, bands - 1)], dst_ref=fin_air.at[landing],
            send_sem=fin_air_send.at[k], recv_sem=fin_air_recv.at[landing],
            device_id={"sec": to}, device_id_type=MESH,
        )

    for k in range(1, members):
        to, copy = air_copy(k, member)
        pl.when(to < bands)(copy.start)

    sea_out[member] = fin_sea_src[...]
    for k in range(1, members):
        origin = lax.rem(member + k, members)
        pltpu.make_async_remote_copy(
            src_ref=fin_sea_src, dst_ref=fin_sea.at[origin],
            send_sem=fin_sea_send.at[k], recv_sem=fin_sea_recv.at[origin],
            device_id={"sec": base + origin}, device_id_type=MESH,
        ).wait_recv()
        sea_out[origin] = fin_sea[origin]

    @pl.when(sec == bands)
    def _():
        air_out[...] = atm_ref[...]

    @pl.when(in_band)
    def _():
        air_out[member] = fin_air_src[jnp.minimum(sec, bands - 1)]
        for k in range(1, members):
            origin = lax.rem(member + k, members)
            air_copy(k, origin)[1].wait_recv()
            air_out[origin] = fin_air[origin]

    for copy in sea_copies:
        copy.wait_send()
    for k in range(1, members):
        to, copy = air_copy(k, member)
        pl.when(to < bands)(copy.wait_send)
    for slot in slots:
        if slot != home:
            for copy in near_copies(slot):
                copy.wait_send()

    @pl.when(in_band)
    def _():
        band = jnp.minimum(sec, bands - 1)
        each_target(lambda slot, to: atm_copy(slot, to, band).wait_send())

    @pl.when(sec == bands)
    def _():
        each_target(lambda slot, to: edge_copy(slot, to).wait_send())


def taps_first(weight):
    return weight.reshape((-1,) + weight.shape[2:])


def shards(
    atmosphere, ocean_state, fluxes, sea_mask, air_entry, air_middle, air_exit, sea_entry, sea_exit
):
    sp = lax.axis_size("sp")
    sections = lax.axis_size("sec")
    bands = sections - 1
    members, fields, rows, band_cols = atmosphere.shape
    surface, cols = ocean_state.shape[1], ocean_state.shape[3]
    hidden = air_entry.shape[3]
    reach = STEPS * (sum(SEA_DILATIONS) + sum(AIR_DILATIONS))
    window = min(sp, 2 * (-(-reach // rows)) + 1)
    home = (window - 1) // 2
    total = window * rows
    depth = round_up(hidden, 16)
    assert band_cols == LANES and cols == bands * band_cols
    assert sections % members == 0 and total <= LANES and surface == fluxes.shape[1]
    dims = (sp, sections, members, rows, fields, surface, cols, window, home, hidden)
    dma = pltpu.SemaphoreType.DMA
    flat = fields * rows
    flat_sea = surface * rows
    raw = (
        air_entry.reshape(-1, hidden), taps_first(air_middle),
        taps_first(air_exit).transpose(0, 2, 1),
        sea_entry.reshape(-1, hidden), taps_first(sea_exit).transpose(0, 2, 1),
    )
    air_depth = LANES * (3 * (hidden // LANES) + 1)
    tile_cols = max(1, TILE_COLS // cols) * cols
    air, sea = pl.pallas_call(
        functools.partial(kernel, dims),
        out_shape=(
            jax.ShapeDtypeStruct((members, flat, band_cols), BF16),
            jax.ShapeDtypeStruct((members, flat_sea, cols), BF16),
        ),
        in_specs=[pl.BlockSpec(memory_space=pltpu.VMEM)] * 4
        + [pl.BlockSpec(memory_space=pl.ANY)] * 5,
        out_specs=(pl.BlockSpec(memory_space=pltpu.VMEM),) * 2,
        scratch_shapes=[
            pltpu.VMEM((window, bands, flat, LANES), BF16),
            pltpu.VMEM((window, flat_sea, cols), BF16),
            pltpu.VMEM((window, flat_sea, cols), BF16),
            pltpu.VMEM((window, rows, cols), jnp.int32),
            pltpu.VMEM((window, fields + surface, LANES), BF16),
            pltpu.VMEM((members, fields + surface, LANES), BF16),
            pltpu.VMEM((total, fields, cols), F32),
            pltpu.VMEM((total, surface, cols), F32),
            pltpu.VMEM((total, surface, cols), F32),
            pltpu.VMEM((total, surface, cols), F32),
            pltpu.VMEM((fields + surface, LANES), F32),
            pltpu.VMEM((total, 3 * 2 * surface, cols), BF16),
            pltpu.VMEM((total, 3 * (fields + surface), cols), BF16),
            pltpu.VMEM((total, depth, cols), BF16),
            pltpu.VMEM((total, depth, cols), BF16),
            pltpu.VMEM((bands, flat, LANES), F32),
            pltpu.VMEM((bands, flat_sea, LANES), F32),
            pltpu.VMEM((bands, flat, LANES), BF16),
            pltpu.VMEM((members, flat, LANES), BF16),
            pltpu.VMEM((flat_sea, cols), BF16),
            pltpu.VMEM((members, flat_sea, cols), BF16),
            pltpu.VMEM((2, 3 * hidden, tile_cols), F32),
            *[pltpu.VMEM(weight.shape, BF16) for weight in raw],
            pltpu.VMEM((hidden, round_up(9 * (fields + surface), LANES)), BF16),
            pltpu.VMEM((3 * hidden, air_depth), BF16),
            pltpu.VMEM((3 * (fields + surface), air_depth), BF16),
            pltpu.VMEM((hidden, round_up(9 * 2 * surface, LANES)), BF16),
            pltpu.VMEM((3 * surface, air_depth), BF16),
            dma((window, sections)),
            dma((window, bands)),
            dma((window, 3)),
            dma((window, 3)),
            dma((window, sections)),
            dma((window,)),
            dma((members,)),
            dma((members,)),
            dma((members,)),
            dma((members,)),
            dma((len(raw),)),
        ],
        compiler_params=pltpu.CompilerParams(
            collective_id=0, has_side_effects=True, vmem_limit_bytes=63 * 1024 * 1024
        ),
    )(
        atmosphere.reshape(members, flat, band_cols),
        ocean_state.reshape(members, flat_sea, cols),
        fluxes.reshape(members, flat_sea, cols),
        sea_mask,
        *raw,
    )
    return air.reshape(atmosphere.shape), sea.reshape(ocean_state.shape)


def solution(mesh):
    placed = (
        P(("grp", "mb"), None, "sp", "sec"),
        P(("grp", "mb"), None, "sp", None),
        P(("grp", "mb"), None, "sp", None),
        P("sp", None),
        P(),
        P(),
        P(),
        P(),
        P(),
    )
    return jax.shard_map(
        shards,
        mesh=mesh,
        in_specs=placed,
        out_specs=(P(("grp", "mb"), None, "sp", "sec"), P(("grp", "mb"), None, "sp", None)),
        check_vma=False,
    )
```
